128 devices in a mesh: dp: 4 (over y), expert: 32 (over z, x, core).
Axes of the slice: x: 4, y: 4, z: 4, core: 2. Of those that a mesh axis runs over, the one named last changes fastest.
Arguments:
- tokens: bfloat16 [6144, 4096], P(('dp', 'expert')), may hold values from -6 to 6
- out_grad: bfloat16 [6144, 4096], P(('dp', 'expert')), may hold values from -6 to 6
- expert_ids: int32 [6144, 8], P(('dp', 'expert')), may hold values from 0 to 31, all different within a row; in each aligned block of 48 rows (0 to 47, 48 to 95, ...) at most 18 rows name the same one
- route_probs: float32 [6144, 8], P(('dp', 'expert')), may hold values from 0.05 to 1
- w_gate: bfloat16 [32, 4096, 768], P('expert'), may hold values from -0.09375 to 0.09375
- w_up: bfloat16 [32, 4096, 768], P('expert'), may hold values from -0.09375 to 0.09375
- w_down: bfloat16 [32, 768, 4096], P('expert'), may hold values from -0.21875 to 0.21875
Outputs:
- token_grad: bfloat16 [6144, 4096], P(('dp', 'expert'))
- gate_grad: bfloat16 [32, 4096, 768], P('expert', 'dp')
- up_grad: bfloat16 [32, 4096, 768], P('expert', 'dp')
- down_grad: bfloat16 [32, 768, 4096], P('expert', None, 'dp')
The draws below stay inside these ranges and needn't reach their ends.
Inputs may be any that keep to these rules, and one draw needn't show every extreme that they name: `expert_ids`: each token names 8 different experts; among the tokens of one device no expert is named by more than 18 tokens, and some expert reaches 18.
All inputs are finite; a program needn't handle non-finite values.
Results may differ from the reference program's by a relative error of at most 0.0064.
Values may be sent and summed in bfloat16 or wider, within the bound.
No kernel may reach another device: no remote copies, remote signals or barrier semaphores. Data moves between devices by JAX's collectives and lax.ppermute only.
A program may use at most 256 MiB of HBM per device.

```python
import math
import jax
import jax.numpy as jnp
import numpy as np
from jax import lax

D = 4096
FF = 768
TOPK = 8
TOK_DEV = 48
EXPERTS = 32
CAP = 18
TOKENS = 6144
N_DP = 4
N_EXPERT = 32


def level_of(key, shape, pieces, low, largest):
    factor_of, own = 1.0, jax.random.fold_in(key, 6)
    for dim, shards_of in pieces:
        steps = jnp.exp(jax.random.uniform(jax.random.fold_in(own, dim), (shards_of,), jnp.float32, low / len(pieces), largest / len(pieces)))
        factor_of = factor_of * jnp.repeat(steps, shape[dim] // shards_of).reshape([-1 if axis == dim else 1 for axis in range(len(shape))])
    return factor_of


def routed_block(stream_key, own, number, rows, count, top, limit, slope):
    order = jax.random.permutation(stream_key, count)
    heavy_load, usual = portions_of(count, rows * top, limit, slope, True), portions_of(count, rows * top, limit, slope, False)
    places = jnp.arange(count)

    def named(sizes, offset_by):
        used = int((sizes > 0).sum())
        fixed = max(1, used // 4)
        moved = fixed + (places - fixed + offset_by * (used - fixed)) % max(1, count - fixed)
        return jnp.zeros((count,), jnp.int32).at[order[jnp.where(places < fixed, places, moved)]].set(jnp.asarray(sizes, jnp.int32))

    sizes = jnp.where(number % 4 == 0, named(heavy_load, number // 4), named(usual, number - number // 4 - 1))
    mixed = jax.random.permutation(jax.random.fold_in(own, 3), count)
    donor, taker = mixed[0:count // 2 * 2:2], mixed[1:count // 2 * 2:2]
    margin = jnp.minimum(sizes[donor] - 1, limit - sizes[taker]) // 2
    margin = jnp.where((donor == order[0]) | (taker == order[0]) | (sizes[taker] == 0), 0, jnp.maximum(margin, 0))
    moved = jax.random.randint(jax.random.fold_in(own, 4), (count // 2,), 0, 1 << 20) % (margin + 1)
    sizes = sizes.at[donor].add(-moved).at[taker].add(moved)
    members = jnp.searchsorted(jnp.cumsum(sizes), jnp.arange(rows * top), side="right").astype(jnp.int32)
    grid = members.reshape(top, rows).T
    grid = grid[jax.random.permutation(jax.random.fold_in(own, 1), rows)]
    offset_by = jax.random.randint(jax.random.fold_in(own, 2), (rows, 1), 0, top)
    return jnp.take_along_axis(grid, (jnp.arange(top)[None, :] + offset_by) % top, axis=1)


def portions_of(amount, total, most, skew, full):
    weights = [(1 << 20) // math.isqrt(grade ** skew) + 1 for grade in range(1, amount + 1)]
    largest = most if full else min(most, max(-(-total // amount), total * weights[0] // sum(weights)))
    least = 1 if total - largest >= amount - 1 else 0
    given, surplus = [largest] + [least] * (amount - 1), total - largest - least * (amount - 1)
    while surplus > 0:
        movable = [i for i in range(1, amount) if given[i] < largest] or [i for i in range(1, amount) if given[i] < most]
        mass, budget = sum([weights[i] for i in movable]), surplus
        for i in movable:
            addition = min(most - given[i], max(1, budget * weights[i] // mass), surplus)
            given[i] = given[i] + addition
            surplus = surplus - addition
    return np.array(given)


def centred(stream_key, shape, spread, most, split=(), kind=jnp.bfloat16):
    entries = jax.random.normal(stream_key, shape, jnp.float32) * spread
    if len(split) > 0:
        entries = level_of(stream_key, shape, split, -0.22, 0.18) * entries
    return jnp.clip(entries, min=-most, max=most).astype(kind)


def setup_inputs(seed: int = 0) -> dict:
    keys = jax.random.split(jax.random.key(seed), 8)
    tokens = centred(keys[0], (TOKENS, D), 1.0, 6.0, ((0, 128),))
    out_grad = centred(keys[1], (TOKENS, D), 1.0, 6.0, ((0, 128),))
    expert_ids_keys = jax.random.split(jax.random.fold_in(keys[2], 1), TOKENS // TOK_DEV)
    expert_ids_turns = jax.random.permutation(jax.random.fold_in(keys[2], 3), TOKENS // TOK_DEV)
    expert_ids = jax.vmap(lambda own, number: routed_block(jax.random.fold_in(keys[2], 2), own, number, TOK_DEV, EXPERTS, TOPK, CAP, 2))(expert_ids_keys, expert_ids_turns).reshape((TOKENS, TOPK))
    route_probs = jnp.clip(jnp.exp(math.log(1.0) - 2.9957323 * jax.random.uniform(keys[3], (TOKENS, TOPK), jnp.float32) ** level_of(keys[3], (TOKENS, TOPK), ((0, 128),), -0.2, 0.2)), 0.05, 1.0)
    w_gate = centred(keys[4], (EXPERTS, D, FF), D ** -0.5, 0.09375, ((0, 32),))
    w_up = centred(keys[5], (EXPERTS, D, FF), D ** -0.5, 0.09375, ((0, 32),))
    w_down = centred(keys[6], (EXPERTS, FF, D), FF ** -0.5, 0.21875, ((0, 32),))
    return dict(tokens=tokens, out_grad=out_grad, expert_ids=expert_ids, route_probs=route_probs, w_gate=w_gate, w_up=w_up, w_down=w_down)


def reference(tokens, out_grad, expert_ids, route_probs, w_gate, w_up, w_down):
    total = tokens.shape[0]
    nrows = total * TOPK
    ids = expert_ids.reshape(nrows).astype(jnp.int32)
    probs = route_probs.reshape(nrows)
    order = jnp.argsort(ids, stable=True).astype(jnp.int32)
    counts = jnp.sum((ids[:, None] == jnp.arange(EXPERTS, dtype=jnp.int32)[None, :]).astype(jnp.int32), axis=0)
    starts = jnp.cumsum(counts) - counts
    window = N_DP * N_EXPERT * CAP

    def per_expert(acc, expert):
        offsets = jnp.arange(window, dtype=jnp.int32)
        valid = offsets < counts[expert]
        rows = order[jnp.minimum(starts[expert] + offsets, nrows - 1)]
        owner = (rows // TOPK).astype(jnp.int32)
        inputs = jnp.where(valid[:, None], tokens[owner], jnp.zeros((), tokens.dtype))
        scaled = jnp.where(valid[:, None], out_grad[owner].astype(jnp.float32) * probs[rows][:, None], 0.0).astype(jnp.bfloat16)
        wgate = w_gate[expert]
        wup = w_up[expert]
        wdown = w_down[expert]
        gate = jnp.dot(inputs, wgate, preferred_element_type=jnp.float32)
        upval = jnp.dot(inputs, wup, preferred_element_type=jnp.float32)
        sgate = jax.nn.silu(gate)
        hidden = (sgate * upval).astype(jnp.bfloat16)
        dhidden = jnp.dot(scaled, wdown.T, preferred_element_type=jnp.float32)
        sigma = jax.nn.sigmoid(gate)
        dgate = (dhidden * upval * sigma * (1.0 + gate * (1.0 - sigma))).astype(jnp.bfloat16)
        dup = (dhidden * sgate).astype(jnp.bfloat16)
        row_grad = (jnp.dot(dgate, wgate.T, preferred_element_type=jnp.float32)
                    + jnp.dot(dup, wup.T, preferred_element_type=jnp.float32)).astype(jnp.bfloat16)
        acc = acc.at[owner].add(jnp.where(valid[:, None], row_grad.astype(acc.dtype), 0.0))
        ggrad = jnp.dot(inputs.T, dgate, preferred_element_type=jnp.float32).astype(jnp.bfloat16)
        ugrad = jnp.dot(inputs.T, dup, preferred_element_type=jnp.float32).astype(jnp.bfloat16)
        dgrad = jnp.dot(hidden.T, scaled, preferred_element_type=jnp.float32).astype(jnp.bfloat16)
        return acc, (ggrad, ugrad, dgrad)

    start = jnp.zeros((total, tokens.shape[1]), jnp.float32)
    acc, (gate_grad, up_grad, down_grad) = lax.scan(per_expert, start, jnp.arange(EXPERTS, dtype=jnp.int32))
    return acc.astype(jnp.bfloat16), gate_grad, up_grad, down_grad
```

```python
import functools

import jax
import jax.numpy as jnp
from jax import lax
from jax.experimental import pallas as pl
from jax.experimental.pallas import tpu as pltpu
from jax.sharding import PartitionSpec as P

BF16 = jnp.bfloat16
F32 = jnp.float32
OFFSETS = (0, -1, 1, 2)
NT = (((1,), (1,)), ((), ()))
TN = (((0,), (0,)), ((), ()))
NN = (((1,), (0,)), ((), ()))


def dot(a, b, dims=NN):
    return lax.dot_general(a, b, dims, preferred_element_type=F32)


def expert_pairs(ring, shift):
    pairs = []
    for e in range(32):
        z, x, c = e // 8, (e // 2) % 4, e % 2
        if (ring == 1) == (c == 0):
            dst = ((z + shift) % 4) * 8 + x * 2 + c
        else:
            dst = z * 8 + ((x + shift) % 4) * 2 + c
        pairs.append((e, dst))
    return pairs


def step(v, ring, shift):
    return lax.ppermute(v, "expert", expert_pairs(ring, shift))


def swap_core(v):
    return lax.ppermute(v, "expert", [(e, e ^ 1) for e in range(32)])


def ring_blocks(v, ring):
    before = step(v, ring, 1)
    after = step(v, ring, -1)
    far0 = step(before[0], ring, 1)
    far1 = step(after[1], ring, -1)
    return v, before, after, far0, far1


def ring_stack(v, ring):
    own, before, after, far0, far1 = ring_blocks(v, ring)
    far = jnp.stack([far0, far1])
    return jnp.concatenate([own, before, after, far], axis=-2)


def plane_gather(v):
    return ring_blocks(ring_stack(v, 1), 2)


def ring_reduce(parts, ring):
    own, before, after, far = parts
    half = far.shape[-1] // 2
    got_b = step(far[..., :half], ring, -1)
    got_a = step(far[..., half:], ring, 1)

    def add(a, b):
        return (a.astype(F32) + b.astype(F32)).astype(BF16)

    before = jnp.concatenate([add(before[..., :half], got_b), before[..., half:]], axis=-1)
    after = jnp.concatenate([after[..., :half], add(after[..., half:], got_a)], axis=-1)
    from_after = step(before, ring, -1)
    from_before = step(after, ring, 1)
    total = own.astype(F32) + from_after.astype(F32) + from_before.astype(F32)
    return total


def tile_of(t, core, half):
    return jnp.where(t < half, core * half + t, (1 - core) * half + t - half)


def forward_kernel(
    place, slot_own, slot_sib, prob, o0, o1, o2, ox, oy, s0, s1, s2, sx, sy, wg, wu, wd,
    h_ref, xi_ref, yi_ref, hot_own, hot_sib, prob_row, xs, ys, gate, up, dh, *, half, cap,
):
    t = pl.program_id(0)
    core, grp = place[0], place[1]
    rows = gate.shape[0]
    part = rows // 4
    width = xs.shape[1]

    @pl.when(t == 0)
    def _():
        total = jnp.zeros((rows, 1), F32)
        for p in range(4):
            r = lax.broadcasted_iota(jnp.int32, (part, slot_own.shape[1]), 0) + part * p
            hit = slot_own[p : p + 1, :] == r
            hot_own[p] = jnp.where(hit, 1.0, 0.0).astype(BF16)
            prob_row[part * p : part * (p + 1), :] = jnp.sum(
                jnp.where(hit, prob[p : p + 1, :], 0.0), axis=1, keepdims=True
            )
            r = lax.broadcasted_iota(jnp.int32, (rows, slot_own.shape[1]), 0)
            hot_sib[p] = jnp.where(slot_sib[p : p + 1, :] == r, 1.0, 0.0).astype(BF16)
        gate[...] = jnp.zeros_like(gate)
        up[...] = jnp.zeros_like(up)
        dh[...] = jnp.zeros_like(dh)

    @pl.when(t < half)
    def _():
        blocks = ((o0[0], o0[1]), (o1[0], o1[1]), (o2[0], o2[1]), (ox[...], oy[...]))
        for p, (bx, by) in enumerate(blocks):
            xs[part * p : part * (p + 1), :] = dot(hot_own[p], bx)
            ys[part * p : part * (p + 1), :] = dot(hot_own[p], by)

    @pl.when(t >= half)
    def _():
        blocks = ((s0[0], s0[1]), (s1[0], s1[1]), (s2[0], s2[1]), (sx[...], sy[...]))
        ax = ay = None
        for p, (bx, by) in enumerate(blocks):
            dx, dy = dot(hot_sib[p], bx), dot(hot_sib[p], by)
            ax, ay = (dx, dy) if ax is None else (ax + dx, ay + dy)
        xs[...] = ax
        ys[...] = ay

    xg = xs[...].astype(BF16)
    yg = (ys[...] * prob_row[...]).astype(BF16)
    gate[...] += dot(xg, wg[...])
    up[...] += dot(xg, wu[...])
    dh[...] += dot(yg, wd[...], NT)
    per_group = 2 * half // 4
    rel = tile_of(t, core, half) - grp * per_group

    @pl.when((rel >= 0) & (rel < per_group))
    def _():
        at = pl.ds(pl.multiple_of(rel * width, width), width)
        xi_ref[:, at] = xg
        yi_ref[:, at] = yg

    @pl.when(t == 2 * half - 1)
    def _():
        ff = gate.shape[1]
        g, u, d = gate[...], up[...], dh[...]
        s = jax.nn.sigmoid(g)
        sg = g * s
        h_ref[:, 0:ff] = (d * u * s * (1.0 + g * (1.0 - s))).astype(BF16)
        h_ref[:, ff : 2 * ff] = (d * sg).astype(BF16)
        h_ref[:, 2 * ff :] = (sg * u).astype(BF16)


def forward(place, slot_own, slot_sib, prob, own, sib, wg, wu, wd, rows, cap):
    width, ff = wg.shape
    half = 4
    tile = width // (2 * half)
    toks = slot_own.shape[1]

    def own_t(t):
        return jnp.minimum(t, half - 1)

    def sib_t(t):
        return jnp.maximum(t - half, 0)

    full = lambda a: pl.BlockSpec(a.shape, lambda t, s: (0,) * a.ndim)
    big_own = pl.BlockSpec((2, toks, tile), lambda t, s: (0, 0, own_t(t)))
    one_own = pl.BlockSpec((toks, tile), lambda t, s: (0, own_t(t)))
    big_sib = pl.BlockSpec((2, toks, tile), lambda t, s: (0, 0, sib_t(t)))
    one_sib = pl.BlockSpec((toks, tile), lambda t, s: (0, sib_t(t)))
    w_in = pl.BlockSpec((tile, ff), lambda t, s: (tile_of(t, s[0], half), 0))
    w_out = pl.BlockSpec((ff, tile), lambda t, s: (0, tile_of(t, s[0], half)))
    flops = 2 * rows * width * ff * 3 + 2 * rows * 4 * toks * width * 2
    return pl.pallas_call(
        functools.partial(forward_kernel, half=half, cap=cap),
        grid_spec=pltpu.PrefetchScalarGridSpec(
            num_scalar_prefetch=1,
            grid=(2 * half,),
            in_specs=[full(slot_own), full(slot_sib), full(prob)]
            + [big_own] * 3 + [one_own] * 2 + [big_sib] * 3 + [one_sib] * 2
            + [w_in, w_in, w_out],
            out_specs=[
                pl.BlockSpec((rows, 3 * ff), lambda t, s: (0, 0)),
                pl.BlockSpec((rows, width // 4), lambda t, s: (0, 0)),
                pl.BlockSpec((rows, width // 4), lambda t, s: (0, 0)),
            ],
            scratch_shapes=[
                pltpu.VMEM((4, rows // 4, toks), BF16),
                pltpu.VMEM((4, rows, toks), BF16),
                pltpu.VMEM((rows, 1), F32),
                pltpu.VMEM((rows, tile), F32),
                pltpu.VMEM((rows, tile), F32),
                pltpu.VMEM((rows, ff), F32),
                pltpu.VMEM((rows, ff), F32),
                pltpu.VMEM((rows, ff), F32),
            ],
        ),
        out_shape=[
            jax.ShapeDtypeStruct((rows, 3 * ff), BF16),
            jax.ShapeDtypeStruct((rows, width // 4), BF16),
            jax.ShapeDtypeStruct((rows, width // 4), BF16),
        ],
        compiler_params=pltpu.CompilerParams(vmem_limit_bytes=36 * 2**20),
        cost_estimate=pl.CostEstimate(
            flops=flops, bytes_accessed=3 * 2 * width * ff + 16 * toks * width, transcendentals=0
        ),
        name="forward",
    )(place, slot_own, slot_sib, prob, *own, *sib, wg, wu, wd)


def rowgrad_kernel(place, slot_own, slot_sib, h, wg, wu, own_ref, sib_ref, hot_own, hot_sib, *, half):
    t = pl.program_id(0)
    rows, ff = h.shape[0], h.shape[1] // 2
    toks = slot_own.shape[1]

    @pl.when(t == 0)
    def _():
        for p in range(4):
            r = lax.broadcasted_iota(jnp.int32, (toks, rows), 1)
            hot_own[p] = jnp.where(slot_own[p] == r, 1.0, 0.0).astype(BF16)
            hot_sib[p] = jnp.where(slot_sib[p] == r, 1.0, 0.0).astype(BF16)

    grad = dot(h[:, 0:ff], wg[...], NT) + dot(h[:, ff:], wu[...], NT)
    grad = grad.astype(BF16)

    @pl.when(t < half)
    def _():
        for p in range(4):
            own_ref[p] = dot(hot_own[p], grad).astype(BF16)

    @pl.when(t >= half)
    def _():
        for p in range(4):
            sib_ref[p] = dot(hot_sib[p], grad).astype(BF16)


def rowgrad(place, slot_own, slot_sib, h, wg, wu):
    width, ff = wg.shape
    rows = h.shape[0]
    half = 4
    tile = width // (2 * half)
    toks = slot_own.shape[1]
    full = lambda a: pl.BlockSpec(a.shape, lambda t, s: (0,) * a.ndim)
    w_in = pl.BlockSpec((tile, ff), lambda t, s: (tile_of(t, s[0], half), 0))
    shape = jax.ShapeDtypeStruct((4, toks, width // 2), BF16)
    return pl.pallas_call(
        functools.partial(rowgrad_kernel, half=half),
        grid_spec=pltpu.PrefetchScalarGridSpec(
            num_scalar_prefetch=1,
            grid=(2 * half,),
            in_specs=[
                full(slot_own), full(slot_sib),
                pl.BlockSpec((rows, 2 * ff), lambda t, s: (0, 0)), w_in, w_in,
            ],
            out_specs=[
                pl.BlockSpec((4, toks, tile), lambda t, s: (0, 0, jnp.minimum(t, half - 1))),
                pl.BlockSpec((4, toks, tile), lambda t, s: (0, 0, jnp.maximum(t - half, 0))),
            ],
            scratch_shapes=[
                pltpu.VMEM((4, toks, rows), BF16),
                pltpu.VMEM((4, toks, rows), BF16),
            ],
        ),
        out_shape=[shape, shape],
        compiler_params=pltpu.CompilerParams(vmem_limit_bytes=36 * 2**20),
        cost_estimate=pl.CostEstimate(
            flops=2 * rows * width * ff * 2 + 2 * rows * 4 * toks * width,
            bytes_accessed=2 * 2 * width * ff + 8 * toks * width,
            transcendentals=0,
        ),
        name="rowgrad",
    )(place, slot_own, slot_sib, h, wg, wu)


def weight_kernel(
    place, slot_own, slot_sib, prob, xi0, yi0, xi1, yi1, h0, h1,
    o0, o1, o2, ox, oy, s0, s1, s2, sx, sy,
    gate_ref, up_ref, down_ref, xs, ys, prob_row, acc_g, acc_u, acc_d,
):
    s = pl.program_id(0)
    core = place[0]
    rows = xi0.shape[0]
    part = rows // 4
    toks = slot_own.shape[-1]
    wide = o0.shape[-1]
    ff = acc_g.shape[1]

    @pl.when(s == 0)
    def _():
        xs[0:rows] = xi0[...]
        xs[rows:] = xi1[...]
        ys[0:rows] = yi0[...]
        ys[rows:] = yi1[...]

    @pl.when(s > 0)
    def _():
        mine = pl.ds(pl.multiple_of(core * wide, wide), wide)
        other = pl.ds(pl.multiple_of((1 - core) * wide, wide), wide)
        for k in range(2):
            base = k * rows
            own = ((o0[0, k, 0], o0[1, k, 0]), (o1[0, k, 0], o1[1, k, 0]), (o2[0, k, 0], o2[1, k, 0]), (ox[k, 0], oy[k, 0]))
            sib = ((s0[0, k, 0], s0[1, k, 0]), (s1[0, k, 0], s1[1, k, 0]), (s2[0, k, 0], s2[1, k, 0]), (sx[k, 0], sy[k, 0]))
            gx, gy, scale = [], [], []
            ax = ay = None
            for p in range(4):
                r = lax.broadcasted_iota(jnp.int32, (part, toks), 0) + part * p
                hit = slot_own[0, k, p : p + 1, :] == r
                scale.append(jnp.sum(jnp.where(hit, prob[0, k, p : p + 1, :], 0.0), axis=1, keepdims=True))
                hot = jnp.where(hit, 1.0, 0.0).astype(BF16)
                gx.append(dot(hot, own[p][0]))
                gy.append(dot(hot, own[p][1]))
                r = lax.broadcasted_iota(jnp.int32, (rows, toks), 0)
                hot = jnp.where(slot_sib[0, k, p : p + 1, :] == r, 1.0, 0.0).astype(BF16)
                dx, dy = dot(hot, sib[p][0]), dot(hot, sib[p][1])
                ax, ay = (dx, dy) if ax is None else (ax + dx, ay + dy)
            for p in range(4):
                prob_row[part * p : part * (p + 1), :] = scale[p]
            scaled = prob_row[...]
            at = slice(base, base + rows)
            xs[at, mine] = jnp.concatenate(gx, axis=0).astype(BF16)
            xs[at, other] = ax.astype(BF16)
            ys[at, mine] = (jnp.concatenate(gy, axis=0) * scaled).astype(BF16)
            ys[at, other] = (ay * scaled).astype(BF16)

    x0, x1 = xs[0:rows], xs[rows:]
    y0, y1 = ys[0:rows], ys[rows:]
    add_g = dot(x0, h0[0, :, 0:ff], TN) + dot(x1, h1[0, :, 0:ff], TN)
    add_u = dot(x0, h0[0, :, ff : 2 * ff], TN) + dot(x1, h1[0, :, ff : 2 * ff], TN)
    add_d = dot(h0[0, :, 2 * ff :], y0, TN) + dot(h1[0, :, 2 * ff :], y1, TN)

    @pl.when(s == 0)
    def _():
        acc_g[...] = add_g
        acc_u[...] = add_u
        acc_d[...] = add_d

    @pl.when((s > 0) & (s < 3))
    def _():
        acc_g[...] += add_g
        acc_u[...] += add_u
        acc_d[...] += add_d

    @pl.when(s == 3)
    def _():
        gate_ref[...] = (acc_g[...] + add_g).astype(BF16)
        up_ref[...] = (acc_u[...] + add_u).astype(BF16)
        down_ref[...] = (acc_d[...] + add_d).astype(BF16)


def weights(place, slot_own, slot_sib, prob, xi, yi, hs, own, sib, ff):
    rows, wide = xi[0].shape
    toks = slot_own.shape[-1]
    cols = wide // 2
    full = lambda a: pl.BlockSpec(a.shape, lambda s, q: (0,) * a.ndim)
    meta = pl.BlockSpec((1, 2, 4, toks), lambda s, q: (s, 0, 0, 0))
    h_spec = pl.BlockSpec((1, rows, 3 * ff), lambda s, q: (lax.rem(q[1] + s, 4), 0, 0))
    big = pl.BlockSpec((2, 2, 1, toks, cols), lambda s, q: (0, 0, jnp.maximum(s - 1, 0), 0, 0))
    one = pl.BlockSpec((2, 1, toks, cols), lambda s, q: (0, jnp.maximum(s - 1, 0), 0, 0))
    return pl.pallas_call(
        weight_kernel,
        grid_spec=pltpu.PrefetchScalarGridSpec(
            num_scalar_prefetch=1,
            grid=(4,),
            in_specs=[meta, meta, meta] + [full(xi[0])] * 4 + [h_spec, h_spec]
            + [big] * 3 + [one] * 2 + [big] * 3 + [one] * 2,
            out_specs=[
                pl.BlockSpec((wide, ff), lambda s, q: (0, 0)),
                pl.BlockSpec((wide, ff), lambda s, q: (0, 0)),
                pl.BlockSpec((ff, wide), lambda s, q: (0, 0)),
            ],
            scratch_shapes=[
                pltpu.VMEM((2 * rows, wide), BF16),
                pltpu.VMEM((2 * rows, wide), BF16),
                pltpu.VMEM((rows, 1), F32),
                pltpu.VMEM((wide, ff), F32),
                pltpu.VMEM((wide, ff), F32),
                pltpu.VMEM((ff, wide), F32),
            ],
        ),
        out_shape=[
            jax.ShapeDtypeStruct((wide, ff), BF16),
            jax.ShapeDtypeStruct((wide, ff), BF16),
            jax.ShapeDtypeStruct((ff, wide), BF16),
        ],
        compiler_params=pltpu.CompilerParams(vmem_limit_bytes=52 * 2**20),
        cost_estimate=pl.CostEstimate(
            flops=2 * 8 * rows * wide * ff * 3 + 2 * 6 * rows * 4 * toks * wide * 2,
            bytes_accessed=8 * rows * 3 * ff * 2 + 24 * 4 * toks * wide,
            transcendentals=0,
        ),
        name="weight_grads",
    )(place, slot_own, slot_sib, prob, xi[0], yi[0], xi[1], yi[1], hs[0], hs[1], *own, *sib)


def on_device(tokens, out_grad, expert_ids, route_probs, w_gate, w_up, w_down):
    toks, width = tokens.shape
    topk = expert_ids.shape[1]
    groups = lax.axis_size("expert")
    cap = 3 * toks * topk // (2 * groups)
    wg, wu, wd = w_gate[0], w_up[0], w_down[0]
    ff = wg.shape[1]
    rows = 16 * cap
    grp = lax.axis_index("dp")
    expert = lax.axis_index("expert")
    z, x, core = expert // 8, (expert // 2) % 4, expert % 2
    first = core == 0
    place = jnp.stack([core, grp]).astype(jnp.int32)

    meta = jnp.concatenate([expert_ids.T.astype(F32), route_probs.T], axis=0)
    meta = lax.all_gather(meta, ("dp", "expert"))
    hit = meta[:, :topk, :] == expert.astype(F32)
    chosen = jnp.any(hit, axis=1)
    prob = jnp.sum(jnp.where(hit, meta[:, topk:, :], 0.0), axis=1)
    lower = jnp.triu(jnp.ones((toks, toks), BF16), 1)
    rank = dot(chosen.astype(BF16), lower).astype(jnp.int32)
    rank = jnp.where(chosen, rank, -(10**6))
    offs = jnp.array(OFFSETS, jnp.int32)
    r2, r1 = offs[:, None], offs[None, :]
    bz = jnp.where(first, z + r1, z + r2) % 4
    bx = jnp.where(first, x + r2, x + r1) % 4
    chip = (bz * 8 + bx * 2).reshape(16)
    dev = (
        ((grp + jnp.arange(4)) % 4)[:, None, None] * 32
        + jnp.arange(2)[None, :, None]
        + chip[None, None, :]
    )
    rank = rank[dev]
    prob = prob[dev].reshape(4, 2, 4, 4 * toks)
    slot = rank + cap * jnp.arange(16, dtype=jnp.int32)[:, None]
    slot_sib = slot.reshape(4, 2, 4, 4, toks).swapaxes(2, 3).reshape(4, 2, 4, 4 * toks)
    slot = slot.reshape(4, 2, 4, 4 * toks)

    both = jnp.stack([tokens, out_grad])

    def by_core(v):
        half = v.shape[-1] // 2
        mine = lax.dynamic_slice_in_dim(v, core * half, half, v.ndim - 1)
        other = lax.dynamic_slice_in_dim(v, (1 - core) * half, half, v.ndim - 1)
        got = swap_core(other)
        return jnp.where(first, mine, got), jnp.where(first, got, mine)

    chunks = by_core(both)

    quarter = width // 4
    other_groups = []
    for g in (1, 2, 3):
        r = 4 - g
        part = lax.dynamic_slice_in_dim(both, ((grp + r) % 4) * quarter, quarter, 2)
        other_groups.append(lax.ppermute(part, "dp", [(s, (s + r) % 4) for s in range(4)]))
    cols = jnp.stack(by_core(jnp.stack(other_groups, axis=1)), axis=1)

    hs, xi, yi, partial = [], [], [], []
    for k in range(2):
        own = plane_gather(chunks[k])
        sib = tuple(swap_core(p) for p in own)
        h, xk, yk = forward(place, slot[0, k], slot_sib[0, k], prob[0, k], own, sib, wg, wu, wd, rows, cap)
        hs.append(lax.all_gather(h, "dp"))
        xi.append(xk)
        yi.append(yk)
        partial.append(rowgrad(place, slot[0, k][..., None], slot_sib[0, k][..., None], h, wg, wu))

    own_c = plane_gather(cols)
    sib_c = tuple(swap_core(p) for p in own_c)

    sums = []
    for mine, other in partial:
        got = swap_core(other)
        total = (mine.astype(F32) + got.astype(F32)).astype(BF16)
        total = ring_reduce([total[p] for p in range(4)], 2).astype(BF16)
        total = total.reshape(4, toks, -1)
        sums.append(ring_reduce([total[p] for p in range(4)], 1).astype(BF16))
    keep = jnp.where(first, sums[0], sums[1])
    got = swap_core(jnp.where(first, sums[1], sums[0]))
    token_grad = jnp.concatenate([jnp.where(first, keep, got), jnp.where(first, got, keep)], axis=1)

    gate_grad, up_grad, down_grad = weights(
        place, slot, slot_sib, prob, xi, yi, hs, own_c, sib_c, ff
    )
    return token_grad, gate_grad[None], up_grad[None], down_grad[None]


def solution(mesh):
    in_specs = (
        P(("dp", "expert"), None),
        P(("dp", "expert"), None),
        P(("dp", "expert"), None),
        P(("dp", "expert"), None),
        P("expert", None, None),
        P("expert", None, None),
        P("expert", None, None),
    )
    out_specs = (
        P(("dp", "expert"), None),
        P("expert", "dp", None),
        P("expert", "dp", None),
        P("expert", None, "dp"),
    )
    return jax.shard_map(
        on_device, mesh=mesh, in_specs=in_specs, out_specs=out_specs, check_vma=False
    )
```

```python
import functools

import jax
import jax.numpy as jnp
from jax import lax
from jax.experimental import pallas as pl
from jax.experimental.pallas import tpu as pltpu
from jax.sharding import PartitionSpec as P

BF16 = jnp.bfloat16
F32 = jnp.float32
OFFSETS = (0, -1, 1, 2)
META_ROWS = 64
HALF = 2
NT = (((1,), (1,)), ((), ()))
TN = (((0,), (0,)), ((), ()))
NN = (((1,), (0,)), ((), ()))


def dot(a, b, dims=NN):
    return lax.dot_general(a, b, dims, preferred_element_type=F32)


def after(v, *events):
    return lax.optimization_barrier((v, events))[0]


def expert_pairs(ring, shift):
    pairs = []
    for e in range(32):
        z, x, c = e // 8, (e // 2) % 4, e % 2
        if (ring == 1) == (c == 0):
            dst = ((z + shift) % 4) * 8 + x * 2 + c
        else:
            dst = z * 8 + ((x + shift) % 4) * 2 + c
        pairs.append((e, dst))
    return pairs


def step(v, ring, shift):
    return lax.ppermute(v, "expert", expert_pairs(ring, shift))


def swap_core(v):
    return lax.ppermute(v, "expert", [(e, e ^ 1) for e in range(32)])


def near(v, ring):
    return step(v, ring, 1), step(v, ring, -1)


def far(prev, succ, ring):
    return step(prev[0], ring, 1), step(succ[1], ring, -1)


def group_gather(h):
    up = [(s, (s + 1) % 4) for s in range(4)]
    down = [(s, (s - 1) % 4) for s in range(4)]
    half = h.shape[0] // 2
    prev = lax.ppermute(h, "dp", up)
    succ = lax.ppermute(h, "dp", down)
    far0 = lax.ppermute(prev[:half], "dp", up)
    far1 = lax.ppermute(succ[half:], "dp", down)
    return [h, succ, far0, far1, prev]


def tile_of(t, core, half):
    return jnp.where(t < half, core * half + t, (1 - core) * half + t - half)


def one_hot(slots, rows):
    r = lax.broadcasted_iota(jnp.int32, (rows, slots.shape[1]), 0)
    return jnp.where(slots == r, 1.0, 0.0).astype(BF16)


def row_probs(slots, prob, rows):
    r = lax.broadcasted_iota(jnp.int32, (rows, slots.shape[1]), 0)
    return jnp.sum(jnp.where(slots == r, prob, 0.0), axis=1, keepdims=True)


def forward_kernel(
    place, slot_own, slot_sib, prob, o0, o1, o2, ox, oy, s0, s1, s2, sx, sy, wg, wu, wd,
    h_ref, xi_ref, yi_ref, hot, prob_row, cat, xs, ys, gate, up, dh, *, half,
):
    t = pl.program_id(0)
    chunks, rows = hot.shape[1], hot.shape[2]
    toks = o0.shape[2]
    width = cat.shape[1]

    @pl.when(t == 0)
    def _():
        for k in range(chunks):
            hot[0, k] = one_hot(slot_own[k], rows)
            hot[1, k] = one_hot(slot_sib[k], rows)
            prob_row[rows * k : rows * (k + 1), :] = row_probs(slot_own[k], prob[k], rows)
        gate[...] = jnp.zeros_like(gate)
        up[...] = jnp.zeros_like(up)
        dh[...] = jnp.zeros_like(dh)

    def gather(side, b0, b1, b2, bx, by):
        for k in range(chunks):
            at = slice(rows * k, rows * (k + 1))
            for v, last in enumerate((bx, by)):
                for p, b in enumerate((b0, b1, b2)):
                    cat[toks * p : toks * (p + 1), :] = b[v, k]
                cat[3 * toks :, :] = last[k]
                got = dot(hot[side, k], cat[...])
                if v == 0:
                    xs[at, :] = got.astype(BF16)
                else:
                    ys[at, :] = (got * prob_row[at, :]).astype(BF16)

    @pl.when(t < half)
    def _():
        gather(0, o0, o1, o2, ox, oy)

    @pl.when(t >= half)
    def _():
        gather(1, s0, s1, s2, sx, sy)

    gate[...] += dot(xs[...], wg[...])
    up[...] += dot(xs[...], wu[...])
    dh[...] += dot(ys[...], wd[...], NT)
    per_group = 2 * half // 4
    rel = tile_of(t, place[0], half) - place[1] * per_group

    @pl.when((rel >= 0) & (rel < per_group))
    def _():
        at = pl.ds(pl.multiple_of(rel * width, width), width)
        xi_ref[:, at] = xs[...]
        yi_ref[:, at] = ys[...]

    @pl.when(t == 2 * half - 1)
    def _():
        ff = gate.shape[1]
        g, u, d = gate[...], up[...], dh[...]
        s = jax.nn.sigmoid(g)
        sg = g * s
        h_ref[:, 0:ff] = (d * u * s * (1.0 + g * (1.0 - s))).astype(BF16)
        h_ref[:, ff : 2 * ff] = (d * sg).astype(BF16)
        h_ref[:, 2 * ff :] = (sg * u).astype(BF16)


def whole(a):
    return pl.BlockSpec(a.shape, lambda *_: (0,) * a.ndim)


def forward(place, slot_own, slot_sib, prob, own, sib, wg, wu, wd, rows, half=4):
    width, ff = wg.shape
    tile = width // (2 * half)
    chunks, toks = own[0].shape[1:3]
    total = chunks * rows

    def own_t(t):
        return jnp.minimum(t, half - 1)

    def sib_t(t):
        return jnp.maximum(t - half, 0)

    big_own = pl.BlockSpec((2, chunks, toks, tile), lambda t, s: (0, 0, 0, own_t(t)))
    one_own = pl.BlockSpec((chunks, toks, tile), lambda t, s: (0, 0, own_t(t)))
    big_sib = pl.BlockSpec((2, chunks, toks, tile), lambda t, s: (0, 0, 0, sib_t(t)))
    one_sib = pl.BlockSpec((chunks, toks, tile), lambda t, s: (0, 0, sib_t(t)))
    w_in = pl.BlockSpec((tile, ff), lambda t, s: (tile_of(t, s[0], half), 0))
    w_out = pl.BlockSpec((ff, tile), lambda t, s: (0, tile_of(t, s[0], half)))
    return pl.pallas_call(
        functools.partial(forward_kernel, half=half),
        grid_spec=pltpu.PrefetchScalarGridSpec(
            num_scalar_prefetch=1,
            grid=(2 * half,),
            in_specs=[whole(slot_own), whole(slot_sib), whole(prob)]
            + [big_own] * 3 + [one_own] * 2 + [big_sib] * 3 + [one_sib] * 2
            + [w_in, w_in, w_out],
            out_specs=[
                pl.BlockSpec((total, 3 * ff), lambda t, s: (0, 0)),
                pl.BlockSpec((total, width // 4), lambda t, s: (0, 0)),
                pl.BlockSpec((total, width // 4), lambda t, s: (0, 0)),
            ],
            scratch_shapes=[
                pltpu.VMEM((2, chunks, rows, 4 * toks), BF16),
                pltpu.VMEM((total, 1), F32),
                pltpu.VMEM((4 * toks, tile), BF16),
                pltpu.VMEM((total, tile), BF16),
                pltpu.VMEM((total, tile), BF16),
                pltpu.VMEM((total, ff), F32),
                pltpu.VMEM((total, ff), F32),
                pltpu.VMEM((total, ff), F32),
            ],
        ),
        out_shape=[
            jax.ShapeDtypeStruct((total, 3 * ff), BF16),
            jax.ShapeDtypeStruct((total, width // 4), BF16),
            jax.ShapeDtypeStruct((total, width // 4), BF16),
        ],
        compiler_params=pltpu.CompilerParams(vmem_limit_bytes=50 * 2**20),
        cost_estimate=pl.CostEstimate(
            flops=2 * total * width * ff * 3 + 2 * total * 4 * toks * width * 2,
            bytes_accessed=3 * 2 * width * ff + 16 * chunks * toks * width,
            transcendentals=0,
        ),
        name="forward",
    )(place, slot_own, slot_sib, prob, *own, *sib, wg, wu, wd)


def rowgrad_kernel(h, wg, wu, out_ref, grad, pieces, *, cap):
    t = pl.program_id(0)
    ff = h.shape[1] // 2
    devices = out_ref.shape[0]
    grad[...] = dot(h[:, 0:ff], wg[...], NT) + dot(h[:, ff:], wu[...], NT)
    for q in range(4):

        @pl.when(t == q)
        def _():
            for n in range(devices):
                at = cap * (n // 2 + devices // 2 * (n % 2))
                pieces[n, cap * q : cap * (q + 1), :] = grad[at : at + cap, :]

    @pl.when(t == 3)
    def _():
        out_ref[...] = pieces[...].astype(BF16)


def rowgrad(h, wg, wu, cap):
    width, ff = wg.shape
    rows = h.shape[0]
    devices, tile = rows // cap, width // 4
    w_in = pl.BlockSpec((tile, ff), lambda t: (t, 0))
    shape = (devices, 4 * cap, tile)
    return pl.pallas_call(
        functools.partial(rowgrad_kernel, cap=cap),
        grid=(4,),
        in_specs=[pl.BlockSpec((rows, 2 * ff), lambda t: (0, 0)), w_in, w_in],
        out_specs=pl.BlockSpec(shape, lambda t: (0, 0, 0)),
        scratch_shapes=[pltpu.VMEM((rows, tile), F32), pltpu.VMEM(shape, F32)],
        out_shape=jax.ShapeDtypeStruct(shape, BF16),
        compiler_params=pltpu.CompilerParams(vmem_limit_bytes=40 * 2**20),
        cost_estimate=pl.CostEstimate(
            flops=2 * rows * width * ff * 2,
            bytes_accessed=2 * 2 * width * ff + 2 * rows * width,
            transcendentals=0,
        ),
        name="rowgrad",
    )(h, wg, wu)


def gather_kernel(slot, prob, xi, yi, blocks, out_ref, cat, xs, ys):
    i, j = pl.program_id(0), pl.program_id(1)
    total, wide = xi.shape
    chips, chunks, toks = blocks.shape[0], blocks.shape[1], blocks.shape[4]
    rows = total // chunks

    @pl.when((i == 0) & (j == 0))
    def _():
        xs[0:total] = xi[...]
        ys[0:total] = yi[...]

    @pl.when((i > 0) | (j > 0))
    def _():
        for k in range(chunks):
            slots = slot[0, k]
            hot = one_hot(slots, rows)
            scale = row_probs(slots, prob[0, k], rows)
            at = pl.ds(pl.multiple_of(j * total + k * rows, rows), rows)
            for n in range(chips):
                cat[toks * n : toks * (n + 1), :] = blocks[n, k, 0, 0]
            xs[at, :] = dot(hot, cat[...]).astype(BF16)
            for n in range(chips):
                cat[toks * n : toks * (n + 1), :] = blocks[n, k, 0, 1]
            ys[at, :] = (dot(hot, cat[...]) * scale).astype(BF16)

    @pl.when(j == 1)
    def _():
        out_ref[0:wide] = xs[...].T
        out_ref[wide:] = ys[...].T


def gather_columns(slot, prob, xi, yi, blocks):
    total, wide = xi.shape
    chips, chunks, _, _, toks, _ = blocks.shape
    meta = pl.BlockSpec((1, chunks, 1, chips * toks), lambda i, j: (2 * i + j, 0, 0, 0))
    return pl.pallas_call(
        gather_kernel,
        grid=(2, 2),
        in_specs=[
            meta, meta, whole(xi), whole(yi),
            pl.BlockSpec(
                (chips, chunks, 1, 2, toks, wide),
                lambda i, j: (0, 0, jnp.maximum(2 * i + j - 1, 0), 0, 0, 0),
            ),
        ],
        out_specs=pl.BlockSpec((2 * wide, 2 * total), lambda i, j: (0, i)),
        scratch_shapes=[
            pltpu.VMEM((chips * toks, wide), BF16),
            pltpu.VMEM((2 * total, wide), BF16),
            pltpu.VMEM((2 * total, wide), BF16),
        ],
        out_shape=jax.ShapeDtypeStruct((2 * wide, 4 * total), BF16),
        compiler_params=pltpu.CompilerParams(vmem_limit_bytes=50 * 2**20),
        cost_estimate=pl.CostEstimate(
            flops=2 * 3 * total * chips * toks * wide * 2,
            bytes_accessed=12 * chunks * chips * toks * wide + 16 * total * wide,
            transcendentals=0,
        ),
        name="gather_columns",
    )(slot, prob, xi, yi, blocks)


def weight_kernel(xy, *refs):
    hs, (gate_ref, up_ref, down_ref, cat) = refs[:-4], refs[-4:]
    m, n = pl.program_id(0), pl.program_id(1)

    @pl.when(n == 0)
    def _():
        at = 0
        for h in hs:
            cat[at : at + h.shape[0], :] = h[...]
            at += h.shape[0]

    res = dot(xy[...], cat[...])

    @pl.when(m == 0)
    def _():
        gate_ref[...] = res.astype(BF16)

    @pl.when(m == 1)
    def _():
        up_ref[...] = res.astype(BF16)

    @pl.when(m == 2)
    def _():
        down_ref[...] = res.astype(BF16).T


def weights(xy, hs, parts=2):
    wide, depth = xy.shape[0] // 2, xy.shape[1]
    ff = hs[0].shape[1] // 3
    bm = wide // parts

    def at(matrix):
        def index(m, n):
            return jnp.where(m == matrix, n, jnp.where(m < matrix, 0, parts - 1))
        return index

    return pl.pallas_call(
        weight_kernel,
        grid=(3, parts),
        in_specs=[pl.BlockSpec((bm, depth), lambda m, n: (jnp.where(m == 2, parts, 0) + n, 0))]
        + [pl.BlockSpec((h.shape[0], ff), lambda m, n: (0, m)) for h in hs],
        out_specs=[
            pl.BlockSpec((bm, ff), lambda m, n: (at(0)(m, n), 0)),
            pl.BlockSpec((bm, ff), lambda m, n: (at(1)(m, n), 0)),
            pl.BlockSpec((ff, bm), lambda m, n: (0, at(2)(m, n))),
        ],
        scratch_shapes=[pltpu.VMEM((depth, ff), BF16)],
        out_shape=[
            jax.ShapeDtypeStruct((wide, ff), BF16),
            jax.ShapeDtypeStruct((wide, ff), BF16),
            jax.ShapeDtypeStruct((ff, wide), BF16),
        ],
        compiler_params=pltpu.CompilerParams(vmem_limit_bytes=52 * 2**20),
        cost_estimate=pl.CostEstimate(
            flops=2 * depth * wide * ff * 3, bytes_accessed=depth * (8 * wide + 6 * ff), transcendentals=0
        ),
        name="weight_grads",
    )(xy, *hs)


def on_device(tokens, out_grad, expert_ids, route_probs, w_gate, w_up, w_down):
    toks, width = tokens.shape
    topk = expert_ids.shape[1]
    groups = lax.axis_size("expert")
    cap = 3 * toks * topk // (2 * groups)
    wg, wu, wd = w_gate[0], w_up[0], w_down[0]
    ff = wg.shape[1]
    rows = 16 * cap
    grp = lax.axis_index("dp")
    expert = lax.axis_index("expert")
    z, x, core = expert // 8, (expert // 2) % 4, expert % 2
    first = core == 0
    place = jnp.stack([core, grp]).astype(jnp.int32)
    both = jnp.stack([tokens, out_grad])

    def by_core(v):
        half = v.shape[-1] // 2
        mine = lax.dynamic_slice_in_dim(v, core * half, half, v.ndim - 1)
        other = lax.dynamic_slice_in_dim(v, (1 - core) * half, half, v.ndim - 1)
        got = swap_core(other)
        return jnp.where(first, mine, got), jnp.where(first, got, mine)

    named = expert_ids[:, :, None] == jnp.arange(groups, dtype=jnp.int32)
    chosen = jnp.any(named, axis=1)
    weight = jnp.sum(jnp.where(named, route_probs[:, :, None], 0.0), axis=1)
    lower = jnp.tril(jnp.ones((toks, toks), BF16), -1)
    rank = jnp.where(chosen, dot(lower, chosen.astype(BF16)), -1000.0)
    meta = jnp.stack([rank.T, weight.T], axis=1).reshape(2 * groups, toks)
    meta = jnp.pad(meta, ((0, META_ROWS - 2 * groups), (0, 128 - toks)))
    meta = lax.all_gather(meta, "expert").reshape(groups, META_ROWS // 2, 2, 128)
    meta = lax.dynamic_slice_in_dim(meta, expert, 1, 1)[:, 0, :, :toks]

    mine = jnp.stack(by_core(both), axis=1)
    col = jnp.concatenate([mine, *near(mine, 1), step(mine, 1, 2)], axis=-2)
    prev, succ = near(col, 2)

    metas = [meta]
    for g in (1, 2, 3):
        r = 4 - g
        metas.append(lax.ppermute(after(meta, col), "dp", [(s, (s + r) % 4) for s in range(4)]))
    metas = jnp.stack(metas).reshape(4, 16, 2, 2, toks)
    base = cap * jnp.arange(16, dtype=jnp.int32)[:, None]
    slots = (metas[:, :, :, 0].astype(jnp.int32) + base[None, :, None]).swapaxes(1, 2)
    slots = slots.reshape(4, 2, 1, 16 * toks)
    probs = metas[:, :, :, 1].swapaxes(1, 2).reshape(4, 2, 1, 16 * toks)
    meta = meta.reshape(16, 2, 2, toks)
    offs = jnp.array(OFFSETS, jnp.int32)
    r2, r1 = offs[:, None], offs[None, :]
    bz = jnp.where(first, z + r1, z + r2) % 4
    bx = jnp.where(first, x + r2, x + r1) % 4
    chip = bz * 4 + bx
    order = jnp.concatenate([chip.reshape(16), chip.T.reshape(16)])
    local = meta[order].reshape(2, 16, 2, 2, toks)
    local_slots = local[:, :, :, 0].astype(jnp.int32) + (cap * order).reshape(2, 16, 1, 1)
    local_slots = local_slots.swapaxes(1, 2).reshape(2, 2, 1, 16 * toks)
    local_probs = local[0, :, :, 1].swapaxes(0, 1).reshape(2, 1, 16 * toks)

    quarter = width // 4
    other_groups = []
    for g in (1, 2, 3):
        r = 4 - g
        part = lax.dynamic_slice_in_dim(after(both, col), ((grp + r) % 4) * quarter, quarter, 2)
        other_groups.append(lax.ppermute(part, "dp", [(s, (s + r) % 4) for s in range(4)]))
    cols = jnp.stack(other_groups).reshape(6 * toks, quarter)
    sib_col = swap_core(col)
    far0, far1 = far(after(prev, cols, metas, sib_col), after(succ, cols, metas, sib_col), 2)
    cols = lax.all_gather(after(cols, far0, far1), "expert", tiled=True)
    cols = cols.reshape(16, 2, 3, 2, toks, quarter)
    early = (sib_col, swap_core(prev), swap_core(succ))
    late = tuple(swap_core(after(p, early)) for p in (far0, far1))
    own, sib = (col, prev, succ, far0, far1), early + late

    h, xi, yi = forward(
        place, local_slots[0], local_slots[1], local_probs, own, sib, wg, wu, wd, rows
    )
    hs = group_gather(h)
    back = lax.all_to_all(rowgrad(h, wg, wu, cap), "expert", 0, 0, tiled=True)
    slots = after(slots, hs[1], hs[4])
    xy = gather_columns(slots, probs, xi, yi, cols)
    gate_grad, up_grad, down_grad = weights(xy, hs)
    back = after(back, gate_grad)
    piece = cap * jnp.arange(4, dtype=F32)
    pick = rank + piece[:, None, None]
    pick = pick[..., None] == jnp.arange(4 * cap, dtype=F32)
    pick = pick.astype(BF16).reshape(4 * toks, groups * 4 * cap)
    token_grad = dot(pick, back.reshape(groups * 4 * cap, quarter)).astype(BF16)
    token_grad = token_grad.reshape(4, toks, quarter).swapaxes(0, 1).reshape(toks, width)

    return token_grad, gate_grad[None], up_grad[None], down_grad[None]


def solution(mesh):
    in_specs = (
        P(("dp", "expert"), None),
        P(("dp", "expert"), None),
        P(("dp", "expert"), None),
        P(("dp", "expert"), None),
        P("expert", None, None),
        P("expert", None, None),
        P("expert", None, None),
    )
    out_specs = (
        P(("dp", "expert"), None),
        P("expert", "dp", None),
        P("expert", "dp", None),
        P("expert", None, "dp"),
    )
    return jax.shard_map(
        on_device, mesh=mesh, in_specs=in_specs, out_specs=out_specs, check_vma=False
    )
```

```python
import functools

import jax
import jax.numpy as jnp
from jax import lax
from jax.experimental import pallas as pl
from jax.experimental.pallas import tpu as pltpu
from jax.sharding import PartitionSpec as P

BF16 = jnp.bfloat16
F32 = jnp.float32
OFFSETS = (0, -1, 1, 2)
HALF = 2
LIGHT = pl.CostEstimate(flops=1, bytes_accessed=1, transcendentals=0)
HEAVY = 4
NT = (((1,), (1,)), ((), ()))
TN = (((0,), (0,)), ((), ()))
NN = (((1,), (0,)), ((), ()))


def dot(a, b, dims=NN):
    return lax.dot_general(a, b, dims, preferred_element_type=F32)


def after(v, *events):
    return lax.optimization_barrier((v, events))[0]


def expert_pairs(ring, shift):
    pairs = []
    for e in range(32):
        z, x, c = e // 8, (e // 2) % 4, e % 2
        if (ring == 1) == (c == 0):
            dst = ((z + shift) % 4) * 8 + x * 2 + c
        else:
            dst = z * 8 + ((x + shift) % 4) * 2 + c
        pairs.append((e, dst))
    return pairs


def step(v, ring, shift):
    return lax.ppermute(v, "expert", expert_pairs(ring, shift))


def swap_core(v):
    return lax.ppermute(v, "expert", [(e, e ^ 1) for e in range(32)])


def near(v, ring):
    return step(v, ring, 1), step(v, ring, -1)


def far(prev, succ, ring):
    return step(prev[0], ring, 1), step(succ[1], ring, -1)


def over_groups(v, shift):
    return lax.ppermute(v, "dp", [(s, (s + shift) % 4) for s in range(4)])


def tile_of(t, core, half):
    return jnp.where(t < half, core * half + t, (1 - core) * half + t - half)


def one_hot(slots, rows):
    r = lax.broadcasted_iota(jnp.int32, (rows, slots.shape[1]), 0)
    return jnp.where(slots == r, 1.0, 0.0).astype(BF16)


def row_probs(slots, prob, rows):
    r = lax.broadcasted_iota(jnp.int32, (rows, slots.shape[1]), 0)
    return jnp.sum(jnp.where(slots == r, prob, 0.0), axis=1, keepdims=True)


def pick_rows(t, half, hot, cat, own, sib, put):
    def gather(side, blocks):
        toks = blocks[0].shape[1]
        for k in range(2):
            for p in range(4):
                cat[toks * p : toks * (p + 1), :] = blocks[4 * k + p][0]
            put(k, dot(hot[side, k], cat[...]))

    @pl.when(t < half)
    def _():
        gather(0, own)

    @pl.when(t >= half)
    def _():
        gather(1, sib)


def keep_columns(t, place, half, rows, out_ref):
    width = rows.shape[1]
    per_group = 2 * half // 4
    rel = tile_of(t, place[0], half) - place[1] * per_group

    @pl.when((rel >= 0) & (rel < per_group))
    def _():
        out_ref[:, pl.ds(pl.multiple_of(rel * width, width), width)] = rows[...]


def hidden_kernel(place, slot_own, slot_sib, *refs, half):
    own, sib = refs[0:8], refs[8:16]
    wg, wu, hid_ref, sg_ref, slope_ref, xi_ref, hot, cat, xs, gate, up = refs[16:]
    t = pl.program_id(0)
    rows = hot.shape[2]

    @pl.when(t == 0)
    def _():
        for k in range(2):
            hot[0, k] = one_hot(slot_own[k], rows)
            hot[1, k] = one_hot(slot_sib[k], rows)
        gate[...] = jnp.zeros_like(gate)
        up[...] = jnp.zeros_like(up)

    def put(k, got):
        xs[rows * k : rows * (k + 1), :] = got.astype(BF16)

    pick_rows(t, half, hot, cat, own, sib, put)
    gate[...] += dot(xs[...], wg[...])
    up[...] += dot(xs[...], wu[...])
    keep_columns(t, place, half, xs, xi_ref)

    @pl.when(t == 2 * half - 1)
    def _():
        g, u = gate[...], up[...]
        s = jax.nn.sigmoid(g)
        sg = g * s
        hid_ref[...] = (sg * u).astype(BF16)
        sg_ref[...] = sg
        slope_ref[...] = u * s * (1.0 + g * (1.0 - s))


def cotangent_kernel(place, slot_own, slot_sib, prob, *refs, half):
    own, sib = refs[0:8], refs[8:16]
    wd, sg, slope, dd_ref, yi_ref, hot, prob_row, cat, ys, dh = refs[16:]
    t = pl.program_id(0)
    rows = hot.shape[2]

    @pl.when(t == 0)
    def _():
        for k in range(2):
            hot[0, k] = one_hot(slot_own[k], rows)
            hot[1, k] = one_hot(slot_sib[k], rows)
            prob_row[rows * k : rows * (k + 1), :] = row_probs(slot_own[k], prob[k], rows)
        dh[...] = jnp.zeros_like(dh)

    def put(k, got):
        at = slice(rows * k, rows * (k + 1))
        ys[at, :] = (got * prob_row[at, :]).astype(BF16)

    pick_rows(t, half, hot, cat, own, sib, put)
    dh[...] += dot(ys[...], wd[...], NT)
    keep_columns(t, place, half, ys, yi_ref)

    @pl.when(t == 2 * half - 1)
    def _():
        dd_ref[0] = (dh[...] * slope[...]).astype(BF16)
        dd_ref[1] = (dh[...] * sg[...]).astype(BF16)


def whole(a):
    return pl.BlockSpec(a.shape, lambda *_: (0,) * a.ndim)


def ring_specs(own, tile, half):
    def spec(block, at):
        array, index = block
        return pl.BlockSpec((1, array.shape[1], tile), lambda t, s: (index, 0, at(t)))

    here = [spec(b, lambda t: jnp.minimum(t, half - 1)) for b in own]
    return here + [spec(b, lambda t: jnp.maximum(t - half, 0)) for b in own]


def hidden_rows(place, slot_own, slot_sib, own, sib, wg, wu, rows, half=4):
    width, ff = wg.shape
    tile = width // (2 * half)
    toks = own[0][0].shape[1]
    total = 2 * rows
    w_in = pl.BlockSpec((tile, ff), lambda t, s: (tile_of(t, s[0], half), 0))
    const = lambda shape: pl.BlockSpec(shape, lambda t, s: (0,) * len(shape))
    outs = [((total, ff), BF16), ((total, ff), F32), ((total, ff), F32), ((total, width // 4), BF16)]
    return pl.pallas_call(
        functools.partial(hidden_kernel, half=half),
        grid_spec=pltpu.PrefetchScalarGridSpec(
            num_scalar_prefetch=1,
            grid=(2 * half,),
            in_specs=[whole(slot_own), whole(slot_sib)] + ring_specs(own, tile, half) + [w_in, w_in],
            out_specs=[const(shape) for shape, _ in outs],
            scratch_shapes=[
                pltpu.VMEM((2, 2, rows, 4 * toks), BF16),
                pltpu.VMEM((4 * toks, tile), BF16),
                pltpu.VMEM((total, tile), BF16),
                pltpu.VMEM((total, ff), F32),
                pltpu.VMEM((total, ff), F32),
            ],
        ),
        out_shape=[jax.ShapeDtypeStruct(shape, kind) for shape, kind in outs],
        compiler_params=pltpu.CompilerParams(vmem_limit_bytes=56 * 2**20),
        cost_estimate=pl.CostEstimate(
            flops=2 * total * width * ff * 2 + 2 * total * 4 * toks * width,
            bytes_accessed=2 * 2 * width * ff + 16 * toks * width,
            transcendentals=0,
        ),
        name="hidden_rows",
    )(place, slot_own, slot_sib, *(b for b, _ in own + sib), wg, wu)


def cotangent_rows(place, slot_own, slot_sib, prob, own, sib, wd, sg, slope, rows, half=4):
    ff, width = wd.shape
    tile = width // (2 * half)
    toks = own[0][0].shape[1]
    total = 2 * rows
    w_out = pl.BlockSpec((ff, tile), lambda t, s: (0, tile_of(t, s[0], half)))
    const = lambda shape: pl.BlockSpec(shape, lambda t, s: (0,) * len(shape))
    outs = [((2, total, ff), BF16), ((total, width // 4), BF16)]
    return pl.pallas_call(
        functools.partial(cotangent_kernel, half=half),
        grid_spec=pltpu.PrefetchScalarGridSpec(
            num_scalar_prefetch=1,
            grid=(2 * half,),
            in_specs=[whole(slot_own), whole(slot_sib), whole(prob)]
            + ring_specs(own, tile, half) + [w_out, whole(sg), whole(slope)],
            out_specs=[const(shape) for shape, _ in outs],
            scratch_shapes=[
                pltpu.VMEM((2, 2, rows, 4 * toks), BF16),
                pltpu.VMEM((total, 1), F32),
                pltpu.VMEM((4 * toks, tile), BF16),
                pltpu.VMEM((total, tile), BF16),
                pltpu.VMEM((total, ff), F32),
            ],
        ),
        out_shape=[jax.ShapeDtypeStruct(shape, kind) for shape, kind in outs],
        compiler_params=pltpu.CompilerParams(vmem_limit_bytes=56 * 2**20),
        cost_estimate=pl.CostEstimate(
            flops=2 * total * width * ff + 2 * total * 4 * toks * width,
            bytes_accessed=2 * width * ff + 16 * toks * width,
            transcendentals=0,
        ),
        name="cotangent_rows",
    )(place, slot_own, slot_sib, prob, *(b for b, _ in own + sib), wd, sg, slope)


def rowgrad_kernel(h, wg, wu, out_ref, grad, pieces, *, cap):
    t = pl.program_id(0)
    devices = out_ref.shape[0]
    grad[...] = dot(h[0], wg[...], NT) + dot(h[1], wu[...], NT)
    for q in range(4):

        @pl.when(t == q)
        def _():
            for n in range(devices):
                at = cap * (n // 2 + devices // 2 * (n % 2))
                pieces[n, cap * q : cap * (q + 1), :] = grad[at : at + cap, :]

    @pl.when(t == 3)
    def _():
        out_ref[...] = pieces[...].astype(BF16)


def rowgrad(h, wg, wu, cap):
    width, ff = wg.shape
    rows = h.shape[1]
    devices, tile = rows // cap, width // 4
    w_in = pl.BlockSpec((tile, ff), lambda t: (t, 0))
    shape = (devices, 4 * cap, tile)
    return pl.pallas_call(
        functools.partial(rowgrad_kernel, cap=cap),
        grid=(4,),
        in_specs=[whole(h), w_in, w_in],
        out_specs=pl.BlockSpec(shape, lambda t: (0, 0, 0)),
        scratch_shapes=[pltpu.VMEM((rows, tile), F32), pltpu.VMEM(shape, F32)],
        out_shape=jax.ShapeDtypeStruct(shape, BF16),
        compiler_params=pltpu.CompilerParams(vmem_limit_bytes=56 * 2**20),
        cost_estimate=pl.CostEstimate(
            flops=2 * rows * width * ff * 2,
            bytes_accessed=2 * 2 * width * ff + 2 * rows * width,
            transcendentals=0,
        ),
        name="rowgrad",
    )(h, wg, wu)


def gather_kernel(slot, prob, xi, yi, blocks, out_ref, cat, xs, ys):
    i, j = pl.program_id(0), pl.program_id(1)
    total, wide = xi.shape
    chips, chunks, toks = blocks.shape[0], blocks.shape[1], blocks.shape[4]
    rows = total // chunks

    @pl.when((i == 0) & (j == 0))
    def _():
        xs[0:total] = xi[...]
        ys[0:total] = yi[...]

    @pl.when((i > 0) | (j > 0))
    def _():
        for k in range(chunks):
            slots = slot[0, k]
            hot = one_hot(slots, rows)
            scale = row_probs(slots, prob[0, k], rows)
            at = pl.ds(pl.multiple_of(j * total + k * rows, rows), rows)
            for n in range(chips):
                cat[toks * n : toks * (n + 1), :] = blocks[n, k, 0, 0]
            xs[at, :] = dot(hot, cat[...]).astype(BF16)
            for n in range(chips):
                cat[toks * n : toks * (n + 1), :] = blocks[n, k, 0, 1]
            ys[at, :] = (dot(hot, cat[...]) * scale).astype(BF16)

    @pl.when(j == 1)
    def _():
        out_ref[0:wide] = xs[...].T
        out_ref[wide:] = ys[...].T


def gather_columns(slot, prob, xi, yi, blocks):
    total, wide = xi.shape
    chips, chunks, _, _, toks, _ = blocks.shape
    meta = pl.BlockSpec((1, chunks, 1, chips * toks), lambda i, j: (2 * i + j, 0, 0, 0))
    return pl.pallas_call(
        gather_kernel,
        grid=(2, 2),
        in_specs=[
            meta, meta, whole(xi), whole(yi),
            pl.BlockSpec(
                (chips, chunks, 1, 2, toks, wide),
                lambda i, j: (0, 0, jnp.maximum(2 * i + j - 1, 0), 0, 0, 0),
            ),
        ],
        out_specs=pl.BlockSpec((2 * wide, 2 * total), lambda i, j: (0, i)),
        scratch_shapes=[
            pltpu.VMEM((chips * toks, wide), BF16),
            pltpu.VMEM((2 * total, wide), BF16),
            pltpu.VMEM((2 * total, wide), BF16),
        ],
        out_shape=jax.ShapeDtypeStruct((2 * wide, 4 * total), BF16),
        compiler_params=pltpu.CompilerParams(vmem_limit_bytes=56 * 2**20),
        cost_estimate=LIGHT,
        name="gather_columns",
    )(slot, prob, xi, yi, blocks)


def weight_kernel(xy, *refs, count):
    outs, cat = refs[-1 - count : -1], refs[-1]
    m = pl.program_id(0)
    at = 0
    for h in refs[: -1 - count]:
        if h.ndim == 3:
            cat[at : at + h.shape[1], :] = h[0]
            at += h.shape[1]
        else:
            cat[at : at + h.shape[0], :] = h[...]
            at += h.shape[0]
    res = dot(xy[...], cat[...]).astype(BF16)
    for i, out in enumerate(outs):

        @pl.when(m == i)
        def _():
            out[...] = res if out.shape == res.shape else res.T


def weights(xy, side, hs, count, flip):
    wide, depth = xy.shape[0] // 2, xy.shape[1]
    ff = hs[0][0].shape[-1]
    shape = (ff, wide) if flip else (wide, ff)

    def spec(block):
        array, rows, index = block
        if array.ndim == 3:
            return pl.BlockSpec((1, rows, ff), lambda m: (index(m), 0, 0))
        return pl.BlockSpec((rows, ff), lambda m: (index(m), 0))

    return pl.pallas_call(
        functools.partial(weight_kernel, count=count),
        grid=(count,),
        in_specs=[pl.BlockSpec((wide, depth), lambda m: (side, 0))] + [spec(h) for h in hs],
        out_specs=[pl.BlockSpec(shape, lambda m: (0, 0))] * count,
        scratch_shapes=[pltpu.VMEM((depth, ff), BF16)],
        out_shape=[jax.ShapeDtypeStruct(shape, BF16)] * count,
        compiler_params=pltpu.CompilerParams(vmem_limit_bytes=56 * 2**20),
        cost_estimate=pl.CostEstimate(
            flops=HEAVY * 2 * depth * wide * ff * count, bytes_accessed=depth * (2 * wide + 2 * ff * count), transcendentals=0
        ),
        name="weight_grads",
    )(xy, *(h for h, _, _ in hs))


def on_device(tokens, out_grad, expert_ids, route_probs, w_gate, w_up, w_down):
    toks, width = tokens.shape
    topk = expert_ids.shape[1]
    groups = lax.axis_size("expert")
    cap = 3 * toks * topk // (2 * groups)
    wg, wu, wd = w_gate[0], w_up[0], w_down[0]
    ff = wg.shape[1]
    rows = 16 * cap
    grp = lax.axis_index("dp")
    expert = lax.axis_index("expert")
    z, x, core = expert // 8, (expert // 2) % 4, expert % 2
    first = core == 0
    place = jnp.stack([core, grp]).astype(jnp.int32)
    both = jnp.stack([tokens, out_grad])

    def by_core(v):
        half = v.shape[-1] // 2
        mine = lax.dynamic_slice_in_dim(v, core * half, half, v.ndim - 1)
        other = lax.dynamic_slice_in_dim(v, (1 - core) * half, half, v.ndim - 1)
        got = swap_core(other)
        return jnp.where(first, mine, got), jnp.where(first, got, mine)

    named = expert_ids[:, :, None] == jnp.arange(groups, dtype=jnp.int32)
    chosen = jnp.any(named, axis=1)
    weight = jnp.sum(jnp.where(named, route_probs[:, :, None], 0.0), axis=1)
    lower = jnp.tril(jnp.ones((toks, toks), BF16), -1)
    rank = jnp.where(chosen, dot(lower, chosen.astype(BF16)), -1000.0)
    mine = jnp.stack(by_core(both), axis=1)
    blocks = (mine, *near(mine, 1), step(mine, 1, 2))
    col_x, col_y = (jnp.concatenate([b[v] for b in blocks], axis=-2) for v in (0, 1))

    meta = lax.all_to_all(jnp.stack([rank.T, weight.T], axis=1), "expert", 0, 0, tiled=True)
    col_x, col_y = after((col_x, col_y), meta)
    prev_x, succ_x = near(col_x, 2)

    quarter = width // 4
    part0 = lax.reduce_precision(meta[:, 1], 8, 7)
    part1 = lax.reduce_precision(meta[:, 1] - part0, 8, 7)
    part2 = meta[:, 1] - part0 - part1
    words = jnp.stack([meta[:, 0], part0, part1, part2]).astype(BF16)
    lines = words.size // quarter
    words = words.reshape(lines, quarter)
    cols, tables = [], [meta]
    for g in (1, 2, 3):
        r = 4 - g
        part = lax.dynamic_slice_in_dim(after(both, col_x), ((grp + r) % 4) * quarter, quarter, 2)
        part = jnp.concatenate([part.reshape(2 * toks, quarter), words])
        got = over_groups(part, r)
        cols.append(got[: 2 * toks])
        got = got[2 * toks :].reshape(4, groups, toks).astype(F32)
        tables.append(jnp.stack([got[0], got[1] + got[2] + got[3]], axis=1))
    cols = jnp.concatenate(cols)
    tables = jnp.stack(tables).reshape(4, 16, 2, 2, toks)
    base = cap * jnp.arange(16, dtype=jnp.int32)[:, None]
    slots = (tables[:, :, :, 0].astype(jnp.int32) + base[None, :, None]).swapaxes(1, 2)
    slots = slots.reshape(4, 2, 1, 16 * toks)
    probs = tables[:, :, :, 1].swapaxes(1, 2).reshape(4, 2, 1, 16 * toks)

    ready = lambda v: after(v, sib_x, cols)
    sib_x = swap_core(col_x)
    up = step(ready(jnp.concatenate([prev_x[:1], col_y])), 2, 1)
    down = step(ready(jnp.concatenate([succ_x[1:], col_y])), 2, -1)
    far_y = step(up[1:2], 2, 1), step(down[2:], 2, -1)

    def blocks_x(col, prev, succ, up, down):
        return [(col, 0), (prev, 0), (succ, 0), (up, 0), (col, 1), (prev, 1), (succ, 1), (down, 0)]

    def blocks_y(col, up, down, far0, far1):
        return [(col, 0), (up, 1), (down, 1), (far0, 0), (col, 1), (up, 2), (down, 2), (far1, 0)]

    sib_up, sib_down = swap_core(up), swap_core(down)
    own_x = blocks_x(col_x, prev_x, succ_x, up, down)
    sib_x = blocks_x(sib_x, swap_core(prev_x), swap_core(succ_x), sib_up, sib_down)
    own_y = blocks_y(col_y, up, down, *far_y)

    table = meta.reshape(16, 2, 2, toks)
    offs = jnp.array(OFFSETS, jnp.int32)
    r2, r1 = offs[:, None], offs[None, :]
    bz = jnp.where(first, z + r1, z + r2) % 4
    bx = jnp.where(first, x + r2, x + r1) % 4
    chip = bz * 4 + bx
    order = jnp.concatenate([chip.reshape(16), chip.T.reshape(16)])
    local = table[order].reshape(2, 16, 2, 2, toks)
    local_slots = local[:, :, :, 0].astype(jnp.int32) + (cap * order).reshape(2, 16, 1, 1)
    local_slots = local_slots.swapaxes(1, 2).reshape(2, 2, 1, 16 * toks)
    local_probs = local[0, :, :, 1].swapaxes(0, 1).reshape(2, 1, 16 * toks)

    cols = lax.all_gather(after(cols, up, down), "expert", tiled=True)
    cols = cols.reshape(16, 2, 3, 2, toks, quarter)

    hid, sg, slope, xi = hidden_rows(
        place, local_slots[0], local_slots[1], own_x, sib_x, wg, wu, rows
    )
    hid_prev, hid_succ = over_groups(hid, 1), over_groups(hid, -1)
    sib_far = [swap_core(after(b, hid)) for b in far_y]
    sib_y = blocks_y(swap_core(col_y), sib_up, sib_down, *sib_far)
    dd, yi = cotangent_rows(
        after(place, hid), local_slots[0], local_slots[1], local_probs, own_y, sib_y, wd, sg, slope, rows
    )

    half = hid.shape[0] // 2
    flat = dd.reshape(-1, ff)
    from_prev = over_groups(jnp.concatenate([hid_prev[:half], flat]), 1)
    from_succ = over_groups(jnp.concatenate([hid_succ[half:], flat]), -1)
    grad = rowgrad(dd, wg, wu, cap)
    xy = gather_columns(after(slots, grad), probs, xi, yi, cols)
    far_gate = over_groups(after(from_prev, xy)[half : 3 * half], 1)
    far_up = over_groups(after(from_succ, xy)[3 * half :], -1)

    back = lax.all_to_all(grad, "expert", 0, 0, tiled=True)
    at = lambda i: lambda m: i
    hids = [(hid, 2 * half, at(0)), (hid_succ, 2 * half, at(0)), (from_prev, half, at(0)),
            (from_succ, half, at(0)), (hid_prev, 2 * half, at(0))]
    (down_grad,) = weights(xy, 1, hids, 1, True)
    far_dd = jnp.stack(after((far_gate, far_up), down_grad))
    first_half, second_half = (lambda m: 1 + 2 * m), (lambda m: 2 + 2 * m)
    dds = [(dd, 2 * half, lambda m: m), (from_succ, half, first_half), (from_succ, half, second_half),
           (far_dd, 2 * half, lambda m: m), (from_prev, half, first_half), (from_prev, half, second_half)]
    gate_grad, up_grad = weights(xy, 0, dds, 2, False)
    back = after(back, gate_grad)
    piece = cap * jnp.arange(4, dtype=F32)
    pick = after(rank, xy) + piece[:, None, None]
    pick = pick[..., None] == jnp.arange(4 * cap, dtype=F32)
    pick = pick.astype(BF16).reshape(4 * toks, groups * 4 * cap)
    token_grad = dot(pick, back.reshape(groups * 4 * cap, quarter)).astype(BF16)
    token_grad = token_grad.reshape(4, toks, quarter).swapaxes(0, 1).reshape(toks, width)

    return token_grad, gate_grad[None], up_grad[None], down_grad[None]


def solution(mesh):
    in_specs = (
        P(("dp", "expert"), None),
        P(("dp", "expert"), None),
        P(("dp", "expert"), None),
        P(("dp", "expert"), None),
        P("expert", None, None),
        P("expert", None, None),
        P("expert", None, None),
    )
    out_specs = (
        P(("dp", "expert"), None),
        P("expert", "dp", None),
        P("expert", "dp", None),
        P("expert", None, "dp"),
    )
    return jax.shard_map(
        on_device, mesh=mesh, in_specs=in_specs, out_specs=out_specs, check_vma=False
    )
```

```python
import functools

import jax
import jax.numpy as jnp
from jax import lax
from jax.experimental import pallas as pl
from jax.experimental.pallas import tpu as pltpu
from jax.sharding import PartitionSpec as P

BF16 = jnp.bfloat16
F32 = jnp.float32
OFFSETS = (0, -1, 1, 2)
HALF = 2
LIGHT = pl.CostEstimate(flops=1, bytes_accessed=1, transcendentals=0)
HEAVY = 4
NT = (((1,), (1,)), ((), ()))
TN = (((0,), (0,)), ((), ()))
NN = (((1,), (0,)), ((), ()))


def dot(a, b, dims=NN):
    return lax.dot_general(a, b, dims, preferred_element_type=F32)


def after(v, *events):
    return lax.optimization_barrier((v, events))[0]


def expert_pairs(ring, shift):
    pairs = []
    for e in range(32):
        z, x, c = e // 8, (e // 2) % 4, e % 2
        if (ring == 1) == (c == 0):
            dst = ((z + shift) % 4) * 8 + x * 2 + c
        else:
            dst = z * 8 + ((x + shift) % 4) * 2 + c
        pairs.append((e, dst))
    return pairs


def step(v, ring, shift):
    return lax.ppermute(v, "expert", expert_pairs(ring, shift))


def swap_core(v):
    return lax.ppermute(v, "expert", [(e, e ^ 1) for e in range(32)])


def near(v, ring):
    return step(v, ring, 1), step(v, ring, -1)


def far(prev, succ, ring):
    return step(prev[0], ring, 1), step(succ[1], ring, -1)


def over_groups(v, shift):
    return lax.ppermute(v, "dp", [(s, (s + shift) % 4) for s in range(4)])


def tile_of(t, core, half):
    return jnp.where(t < half, core * half + t, (1 - core) * half + t - half)


def one_hot(slots, rows):
    r = lax.broadcasted_iota(jnp.int32, (rows, slots.shape[1]), 0)
    return jnp.where(slots == r, 1.0, 0.0).astype(BF16)


def row_probs(slots, prob, rows):
    r = lax.broadcasted_iota(jnp.int32, (rows, slots.shape[1]), 0)
    return jnp.sum(jnp.where(slots == r, prob, 0.0), axis=1, keepdims=True)


def pick_rows(t, half, hot, cat, own, sib, put):
    def gather(side, blocks):
        toks = blocks[0].shape[1]
        for k in range(2):
            for p in range(4):
                cat[toks * p : toks * (p + 1), :] = blocks[4 * k + p][0]
            put(k, dot(hot[side, k], cat[...]))

    @pl.when(t < half)
    def _():
        gather(0, own)

    @pl.when(t >= half)
    def _():
        gather(1, sib)


def keep_columns(t, place, half, rows, out_ref):
    width = rows.shape[1]
    per_group = 2 * half // 4
    rel = tile_of(t, place[0], half) - place[1] * per_group

    @pl.when((rel >= 0) & (rel < per_group))
    def _():
        out_ref[:, pl.ds(pl.multiple_of(rel * width, width), width)] = rows[...]


def hidden_kernel(place, slot_own, slot_sib, prob, *refs, half):
    own, sib = refs[0:8], refs[8:16]
    wg, wu, hid_ref, sg_ref, slope_ref, xi_ref, hot, scale_ref, cat, xs, gate, up = refs[16:]
    t = pl.program_id(0)
    rows = hot.shape[2]

    @pl.when(t == 0)
    def _():
        for k in range(2):
            hot[0, k] = one_hot(slot_own[k], rows)
            hot[1, k] = one_hot(slot_sib[k], rows)
            scale = row_probs(slot_own[k], prob[k], rows)
            scale_ref[rows * k : rows * (k + 1), :] = jnp.broadcast_to(scale, (rows, 128))
        gate[...] = jnp.zeros_like(gate)
        up[...] = jnp.zeros_like(up)

    def put(k, got):
        xs[rows * k : rows * (k + 1), :] = got.astype(BF16)

    pick_rows(t, half, hot, cat, own, sib, put)
    gate[...] += dot(xs[...], wg[...])
    up[...] += dot(xs[...], wu[...])
    keep_columns(t, place, half, xs, xi_ref)

    @pl.when(t == 2 * half - 1)
    def _():
        g, u = gate[...], up[...]
        s = jax.nn.sigmoid(g)
        sg = g * s
        hid_ref[...] = (sg * u).astype(BF16)
        sg_ref[...] = sg
        slope_ref[...] = u * s * (1.0 + g * (1.0 - s))


def cotangent_kernel(place, hot, scale, *refs, half):
    own, sib = refs[0:8], refs[8:16]
    wd, sg, slope, dd_ref, yi_ref, cat, ys, dh = refs[16:]
    t = pl.program_id(0)
    rows = hot.shape[2]

    @pl.when(t == 0)
    def _():
        dh[...] = jnp.zeros_like(dh)

    def put(k, got):
        at = slice(rows * k, rows * (k + 1))
        ys[at, :] = (got * scale[at, 0:1]).astype(BF16)

    pick_rows(t, half, hot, cat, own, sib, put)
    dh[...] += dot(ys[...], wd[...], NT)
    keep_columns(t, place, half, ys, yi_ref)

    @pl.when(t == 2 * half - 1)
    def _():
        dd_ref[0] = (dh[...] * slope[...]).astype(BF16)
        dd_ref[1] = (dh[...] * sg[...]).astype(BF16)


def whole(a):
    return pl.BlockSpec(a.shape, lambda *_: (0,) * a.ndim)


def ring_specs(own, tile, half):
    def spec(block, at):
        array, index = block
        return pl.BlockSpec((1, array.shape[1], tile), lambda t, s: (index, 0, at(t)))

    here = [spec(b, lambda t: jnp.minimum(t, half - 1)) for b in own]
    return here + [spec(b, lambda t: jnp.maximum(t - half, 0)) for b in own]


def hidden_rows(place, slot_own, slot_sib, prob, own, sib, wg, wu, rows, half=2):
    width, ff = wg.shape
    tile = width // (2 * half)
    toks = own[0][0].shape[1]
    total = 2 * rows
    w_in = pl.BlockSpec((tile, ff), lambda t, s: (tile_of(t, s[0], half), 0))
    const = lambda shape: pl.BlockSpec(shape, lambda t, s: (0,) * len(shape))
    outs = [((total, ff), BF16), ((total, ff), F32), ((total, ff), F32), ((total, width // 4), BF16)]
    outs += [((2, 2, rows, 4 * toks), BF16), ((total, 128), F32)]
    return pl.pallas_call(
        functools.partial(hidden_kernel, half=half),
        grid_spec=pltpu.PrefetchScalarGridSpec(
            num_scalar_prefetch=1,
            grid=(2 * half,),
            in_specs=[whole(slot_own), whole(slot_sib), whole(prob)] + ring_specs(own, tile, half) + [w_in, w_in],
            out_specs=[const(shape) for shape, _ in outs],
            scratch_shapes=[
                pltpu.VMEM((4 * toks, tile), BF16),
                pltpu.VMEM((total, tile), BF16),
                pltpu.VMEM((total, ff), F32),
                pltpu.VMEM((total, ff), F32),
            ],
        ),
        out_shape=[jax.ShapeDtypeStruct(shape, kind) for shape, kind in outs],
        compiler_params=pltpu.CompilerParams(vmem_limit_bytes=56 * 2**20),
        cost_estimate=pl.CostEstimate(
            flops=2 * total * width * ff * 2 + 2 * total * 4 * toks * width,
            bytes_accessed=2 * 2 * width * ff + 16 * toks * width,
            transcendentals=0,
        ),
        name="hidden_rows",
    )(place, slot_own, slot_sib, prob, *(b for b, _ in own + sib), wg, wu)


def cotangent_rows(place, hot, scale, own, sib, wd, sg, slope, rows, half=2):
    ff, width = wd.shape
    tile = width // (2 * half)
    toks = own[0][0].shape[1]
    total = 2 * rows
    w_out = pl.BlockSpec((ff, tile), lambda t, s: (0, tile_of(t, s[0], half)))
    const = lambda shape: pl.BlockSpec(shape, lambda t, s: (0,) * len(shape))
    outs = [((2, total, ff), BF16), ((total, width // 4), BF16)]
    return pl.pallas_call(
        functools.partial(cotangent_kernel, half=half),
        grid_spec=pltpu.PrefetchScalarGridSpec(
            num_scalar_prefetch=1,
            grid=(2 * half,),
            in_specs=[whole(hot), whole(scale)]
            + ring_specs(own, tile, half) + [w_out, whole(sg), whole(slope)],
            out_specs=[const(shape) for shape, _ in outs],
            scratch_shapes=[
                pltpu.VMEM((4 * toks, tile), BF16),
                pltpu.VMEM((total, tile), BF16),
                pltpu.VMEM((total, ff), F32),
            ],
        ),
        out_shape=[jax.ShapeDtypeStruct(shape, kind) for shape, kind in outs],
        compiler_params=pltpu.CompilerParams(vmem_limit_bytes=56 * 2**20),
        cost_estimate=pl.CostEstimate(
            flops=2 * total * width * ff + 2 * total * 4 * toks * width,
            bytes_accessed=2 * width * ff + 16 * toks * width,
            transcendentals=0,
        ),
        name="cotangent_rows",
    )(place, hot, scale, *(b for b, _ in own + sib), wd, sg, slope)


def rowgrad_kernel(h, wg, wu, out_ref, grad, pieces, *, cap):
    t = pl.program_id(0)
    devices = out_ref.shape[0]
    grad[...] = dot(h[0], wg[...], NT) + dot(h[1], wu[...], NT)
    for q in range(4):

        @pl.when(t == q)
        def _():
            for n in range(devices):
                at = cap * (n // 2 + devices // 2 * (n % 2))
                pieces[n, cap * q : cap * (q + 1), :] = grad[at : at + cap, :]

    @pl.when(t == 3)
    def _():
        out_ref[...] = pieces[...].astype(BF16)


def rowgrad(h, wg, wu, cap):
    width, ff = wg.shape
    rows = h.shape[1]
    devices, tile = rows // cap, width // 4
    w_in = pl.BlockSpec((tile, ff), lambda t: (t, 0))
    shape = (devices, 4 * cap, tile)
    return pl.pallas_call(
        functools.partial(rowgrad_kernel, cap=cap),
        grid=(4,),
        in_specs=[whole(h), w_in, w_in],
        out_specs=pl.BlockSpec(shape, lambda t: (0, 0, 0)),
        scratch_shapes=[pltpu.VMEM((rows, tile), F32), pltpu.VMEM(shape, F32)],
        out_shape=jax.ShapeDtypeStruct(shape, BF16),
        compiler_params=pltpu.CompilerParams(vmem_limit_bytes=56 * 2**20),
        cost_estimate=pl.CostEstimate(
            flops=2 * rows * width * ff * 2,
            bytes_accessed=2 * 2 * width * ff + 2 * rows * width,
            transcendentals=0,
        ),
        name="rowgrad",
    )(h, wg, wu)


def gather_kernel(slot, prob, xi, yi, blocks, out_ref, cat, xs, ys):
    i, j = pl.program_id(0), pl.program_id(1)
    total, wide = xi.shape
    chips, chunks, toks = blocks.shape[0], blocks.shape[1], blocks.shape[4]
    rows = total // chunks

    @pl.when((i == 0) & (j == 0))
    def _():
        xs[0:total] = xi[...]
        ys[0:total] = yi[...]

    @pl.when((i > 0) | (j > 0))
    def _():
        for k in range(chunks):
            slots = slot[0, k]
            hot = one_hot(slots, rows)
            scale = row_probs(slots, prob[0, k], rows)
            at = pl.ds(pl.multiple_of(j * total + k * rows, rows), rows)
            for n in range(chips):
                cat[toks * n : toks * (n + 1), :] = blocks[n, k, 0, 0]
            xs[at, :] = dot(hot, cat[...]).astype(BF16)
            for n in range(chips):
                cat[toks * n : toks * (n + 1), :] = blocks[n, k, 0, 1]
            ys[at, :] = (dot(hot, cat[...]) * scale).astype(BF16)

    @pl.when(j == 1)
    def _():
        out_ref[0:wide] = xs[...].T
        out_ref[wide:] = ys[...].T


def gather_columns(slot, prob, xi, yi, blocks):
    total, wide = xi.shape
    chips, chunks, _, _, toks, _ = blocks.shape
    meta = pl.BlockSpec((1, chunks, 1, chips * toks), lambda i, j: (2 * i + j, 0, 0, 0))
    return pl.pallas_call(
        gather_kernel,
        grid=(2, 2),
        in_specs=[
            meta, meta, whole(xi), whole(yi),
            pl.BlockSpec(
                (chips, chunks, 1, 2, toks, wide),
                lambda i, j: (0, 0, jnp.maximum(2 * i + j - 1, 0), 0, 0, 0),
            ),
        ],
        out_specs=pl.BlockSpec((2 * wide, 2 * total), lambda i, j: (0, i)),
        scratch_shapes=[
            pltpu.VMEM((chips * toks, wide), BF16),
            pltpu.VMEM((2 * total, wide), BF16),
            pltpu.VMEM((2 * total, wide), BF16),
        ],
        out_shape=jax.ShapeDtypeStruct((2 * wide, 4 * total), BF16),
        compiler_params=pltpu.CompilerParams(vmem_limit_bytes=56 * 2**20),
        cost_estimate=LIGHT,
        name="gather_columns",
    )(slot, prob, xi, yi, blocks)


def weight_kernel(xy, *refs, count):
    outs, cat = refs[-1 - count : -1], refs[-1]
    m = pl.program_id(0)
    at = 0
    for h in refs[: -1 - count]:
        if h.ndim == 3:
            cat[at : at + h.shape[1], :] = h[0]
            at += h.shape[1]
        else:
            cat[at : at + h.shape[0], :] = h[...]
            at += h.shape[0]
    res = dot(xy[...], cat[...]).astype(BF16)
    for i, out in enumerate(outs):

        @pl.when(m == i)
        def _():
            out[...] = res if out.shape == res.shape else res.T


def weights(xy, side, hs, count, flip):
    wide, depth = xy.shape[0] // 2, xy.shape[1]
    ff = hs[0][0].shape[-1]
    shape = (ff, wide) if flip else (wide, ff)

    def spec(block):
        array, rows, index = block
        if array.ndim == 3:
            return pl.BlockSpec((1, rows, ff), lambda m: (index(m), 0, 0))
        return pl.BlockSpec((rows, ff), lambda m: (index(m), 0))

    return pl.pallas_call(
        functools.partial(weight_kernel, count=count),
        grid=(count,),
        in_specs=[pl.BlockSpec((wide, depth), lambda m: (side, 0))] + [spec(h) for h in hs],
        out_specs=[pl.BlockSpec(shape, lambda m: (0, 0))] * count,
        scratch_shapes=[pltpu.VMEM((depth, ff), BF16)],
        out_shape=[jax.ShapeDtypeStruct(shape, BF16)] * count,
        compiler_params=pltpu.CompilerParams(vmem_limit_bytes=56 * 2**20),
        cost_estimate=pl.CostEstimate(
            flops=HEAVY * 2 * depth * wide * ff * count, bytes_accessed=depth * (2 * wide + 2 * ff * count), transcendentals=0
        ),
        name="weight_grads",
    )(xy, *(h for h, _, _ in hs))


def on_device(tokens, out_grad, expert_ids, route_probs, w_gate, w_up, w_down):
    toks, width = tokens.shape
    topk = expert_ids.shape[1]
    groups = lax.axis_size("expert")
    cap = 3 * toks * topk // (2 * groups)
    wg, wu, wd = w_gate[0], w_up[0], w_down[0]
    ff = wg.shape[1]
    rows = 16 * cap
    grp = lax.axis_index("dp")
    expert = lax.axis_index("expert")
    z, x, core = expert // 8, (expert // 2) % 4, expert % 2
    first = core == 0
    place = jnp.stack([core, grp]).astype(jnp.int32)
    both = jnp.stack([tokens, out_grad])

    def by_core(v):
        half = v.shape[-1] // 2
        mine = lax.dynamic_slice_in_dim(v, core * half, half, v.ndim - 1)
        other = lax.dynamic_slice_in_dim(v, (1 - core) * half, half, v.ndim - 1)
        got = swap_core(other)
        return jnp.where(first, mine, got), jnp.where(first, got, mine)

    named = expert_ids[:, :, None] == jnp.arange(groups, dtype=jnp.int32)
    chosen = jnp.any(named, axis=1)
    weight = jnp.sum(jnp.where(named, route_probs[:, :, None], 0.0), axis=1)
    lower = jnp.tril(jnp.ones((toks, toks), BF16), -1)
    rank = jnp.where(chosen, dot(lower, chosen.astype(BF16)), -1000.0)
    mine = jnp.stack(by_core(both), axis=1)
    blocks = (mine, *near(mine, 1), step(mine, 1, 2))
    col_x, col_y = (jnp.concatenate([b[v] for b in blocks], axis=-2) for v in (0, 1))

    meta = lax.all_to_all(jnp.stack([rank.T, weight.T], axis=1), "expert", 0, 0, tiled=True)
    col_x, col_y = after((col_x, col_y), meta)
    prev_x, succ_x = near(col_x, 2)

    quarter = width // 4
    part0 = lax.reduce_precision(meta[:, 1], 8, 7)
    part1 = lax.reduce_precision(meta[:, 1] - part0, 8, 7)
    part2 = meta[:, 1] - part0 - part1
    words = jnp.stack([meta[:, 0], part0, part1, part2]).astype(BF16)
    lines = words.size // quarter
    words = words.reshape(lines, quarter)
    cols, tables = [], [meta]
    for g in (1, 2, 3):
        r = 4 - g
        part = lax.dynamic_slice_in_dim(after(both, col_x), ((grp + r) % 4) * quarter, quarter, 2)
        part = jnp.concatenate([part.reshape(2 * toks, quarter), words])
        got = over_groups(part, r)
        cols.append(got[: 2 * toks])
        got = got[2 * toks :].reshape(4, groups, toks).astype(F32)
        tables.append(jnp.stack([got[0], got[1] + got[2] + got[3]], axis=1))
    cols = jnp.concatenate(cols)
    tables = jnp.stack(tables).reshape(4, 16, 2, 2, toks)
    base = cap * jnp.arange(16, dtype=jnp.int32)[:, None]
    slots = (tables[:, :, :, 0].astype(jnp.int32) + base[None, :, None]).swapaxes(1, 2)
    slots = slots.reshape(4, 2, 1, 16 * toks)
    probs = tables[:, :, :, 1].swapaxes(1, 2).reshape(4, 2, 1, 16 * toks)

    sib_near = (swap_core(col_x), swap_core(after(prev_x, cols)), swap_core(after(succ_x, cols)))
    ready = lambda v: after(v, sib_near)
    up = step(ready(jnp.concatenate([prev_x[:1], col_y])), 2, 1)
    down = step(ready(jnp.concatenate([succ_x[1:], col_y])), 2, -1)
    far_y = step(up[1:2], 2, 1), step(down[2:], 2, -1)

    def blocks_x(col, prev, succ, up, down):
        return [(col, 0), (prev, 0), (succ, 0), (up, 0), (col, 1), (prev, 1), (succ, 1), (down, 0)]

    def blocks_y(col, up, down, far0, far1):
        return [(col, 0), (up, 1), (down, 1), (far0, 0), (col, 1), (up, 2), (down, 2), (far1, 0)]

    sib_up, sib_down = swap_core(up), swap_core(down)
    own_x = blocks_x(col_x, prev_x, succ_x, up, down)
    sib_x = blocks_x(*sib_near, sib_up, sib_down)
    own_y = blocks_y(col_y, up, down, *far_y)

    table = meta.reshape(16, 2, 2, toks)
    offs = jnp.array(OFFSETS, jnp.int32)
    r2, r1 = offs[:, None], offs[None, :]
    bz = jnp.where(first, z + r1, z + r2) % 4
    bx = jnp.where(first, x + r2, x + r1) % 4
    chip = bz * 4 + bx
    order = jnp.concatenate([chip.reshape(16), chip.T.reshape(16)])
    local = table[order].reshape(2, 16, 2, 2, toks)
    local_slots = local[:, :, :, 0].astype(jnp.int32) + (cap * order).reshape(2, 16, 1, 1)
    local_slots = local_slots.swapaxes(1, 2).reshape(2, 2, 1, 16 * toks)
    local_probs = local[0, :, :, 1].swapaxes(0, 1).reshape(2, 1, 16 * toks)

    cols = lax.all_gather(after(cols, up, down), "expert", tiled=True)
    cols = cols.reshape(16, 2, 3, 2, toks, quarter)

    hid, sg, slope, xi, hot, scale = hidden_rows(
        place, local_slots[0], local_slots[1], local_probs, own_x, sib_x, wg, wu, rows
    )
    hid_prev, hid_succ = over_groups(hid, 1), over_groups(hid, -1)
    sib_far = [swap_core(after(b, hid)) for b in far_y]
    sib_y = blocks_y(swap_core(col_y), sib_up, sib_down, *sib_far)
    dd, yi = cotangent_rows(
        place, hot, scale, own_y, sib_y, wd, sg, slope, rows
    )

    half = hid.shape[0] // 2
    flat = dd.reshape(-1, ff)
    from_prev = over_groups(jnp.concatenate([hid_prev[:half], flat]), 1)
    from_succ = over_groups(jnp.concatenate([hid_succ[half:], flat]), -1)
    grad = rowgrad(dd, wg, wu, cap)
    xy = gather_columns(after(slots, grad), probs, xi, yi, cols)
    far_gate = over_groups(after(from_prev, xy)[half : 3 * half], 1)
    far_up = over_groups(after(from_succ, xy)[3 * half :], -1)

    back = lax.all_to_all(grad, "expert", 0, 0, tiled=True)
    at = lambda i: lambda m: i
    hids = [(hid, 2 * half, at(0)), (hid_succ, 2 * half, at(0)), (from_prev, half, at(0)),
            (from_succ, half, at(0)), (hid_prev, 2 * half, at(0))]
    (down_grad,) = weights(xy, 1, hids, 1, True)
    far_dd = jnp.stack(after((far_gate, far_up), down_grad))
    first_half, second_half = (lambda m: 1 + 2 * m), (lambda m: 2 + 2 * m)
    dds = [(dd, 2 * half, lambda m: m), (from_succ, half, first_half), (from_succ, half, second_half),
           (far_dd, 2 * half, lambda m: m), (from_prev, half, first_half), (from_prev, half, second_half)]
    gate_grad, up_grad = weights(xy, 0, dds, 2, False)
    back = after(back, gate_grad)
    piece = cap * jnp.arange(4, dtype=F32)
    pick = after(rank, xy) + piece[:, None, None]
    pick = pick[..., None] == jnp.arange(4 * cap, dtype=F32)
    pick = pick.astype(BF16).reshape(4 * toks, groups * 4 * cap)
    token_grad = dot(pick, back.reshape(groups * 4 * cap, quarter)).astype(BF16)
    token_grad = token_grad.reshape(4, toks, quarter).swapaxes(0, 1).reshape(toks, width)

    return token_grad, gate_grad[None], up_grad[None], down_grad[None]


def solution(mesh):
    in_specs = (
        P(("dp", "expert"), None),
        P(("dp", "expert"), None),
        P(("dp", "expert"), None),
        P(("dp", "expert"), None),
        P("expert", None, None),
        P("expert", None, None),
        P("expert", None, None),
    )
    out_specs = (
        P(("dp", "expert"), None),
        P("expert", "dp", None),
        P("expert", "dp", None),
        P("expert", None, "dp"),
    )
    return jax.shard_map(
        on_device, mesh=mesh, in_specs=in_specs, out_specs=out_specs, check_vma=False
    )
```

```python
import functools

import jax
import jax.numpy as jnp
from jax import lax
from jax.experimental import pallas as pl
from jax.experimental.pallas import tpu as pltpu
from jax.sharding import PartitionSpec as P

BF16 = jnp.bfloat16
F32 = jnp.float32
OFFSETS = (0, -1, 1, 2)
HALF = 2
LIGHT = pl.CostEstimate(flops=1, bytes_accessed=1, transcendentals=0)
HEAVY = 4
NT = (((1,), (1,)), ((), ()))
TN = (((0,), (0,)), ((), ()))
NN = (((1,), (0,)), ((), ()))


def dot(a, b, dims=NN):
    return lax.dot_general(a, b, dims, preferred_element_type=F32)


def after(v, *events):
    return lax.optimization_barrier((v, events))[0]


def expert_pairs(ring, shift):
    pairs = []
    for e in range(32):
        z, x, c = e // 8, (e // 2) % 4, e % 2
        if (ring == 1) == (c == 0):
            dst = ((z + shift) % 4) * 8 + x * 2 + c
        else:
            dst = z * 8 + ((x + shift) % 4) * 2 + c
        pairs.append((e, dst))
    return pairs


def step(v, ring, shift):
    return lax.ppermute(v, "expert", expert_pairs(ring, shift))


def swap_core(v):
    return lax.ppermute(v, "expert", [(e, e ^ 1) for e in range(32)])


def near(v, ring):
    return step(v, ring, 1), step(v, ring, -1)


def far(prev, succ, ring):
    return step(prev[0], ring, 1), step(succ[1], ring, -1)


def over_groups(v, shift):
    return lax.ppermute(v, "dp", [(s, (s + shift) % 4) for s in range(4)])


def tile_of(t, core, half):
    return jnp.where(t < half, core * half + t, (1 - core) * half + t - half)


def one_hot(slots, rows):
    r = lax.broadcasted_iota(jnp.int32, (rows, slots.shape[1]), 0)
    return jnp.where(slots == r, 1.0, 0.0).astype(BF16)


def row_probs(slots, prob, rows):
    r = lax.broadcasted_iota(jnp.int32, (rows, slots.shape[1]), 0)
    return jnp.sum(jnp.where(slots == r, prob, 0.0), axis=1, keepdims=True)


def pick_rows(t, half, hot, cat, own, sib, put):
    def gather(side, blocks):
        toks = blocks[0].shape[1]
        for k in range(2):
            for p in range(4):
                cat[toks * p : toks * (p + 1), :] = blocks[4 * k + p][0]
            put(k, dot(hot[side, k], cat[...]))

    @pl.when(t < half)
    def _():
        gather(0, own)

    @pl.when(t >= half)
    def _():
        gather(1, sib)


def keep_columns(t, place, half, rows, out_ref):
    width = rows.shape[1]
    per_group = 2 * half // 4
    rel = tile_of(t, place[0], half) - place[1] * per_group

    @pl.when((rel >= 0) & (rel < per_group))
    def _():
        out_ref[:, pl.ds(pl.multiple_of(rel * width, width), width)] = rows[...]


def hidden_kernel(place, slot_own, slot_sib, prob, *refs, half):
    own, sib = refs[0:8], refs[8:16]
    wg, wu, hid_ref, sg_ref, slope_ref, xi_ref, hot, scale_ref, cat, xs, gate, up = refs[16:]
    t = pl.program_id(0)
    rows = hot.shape[2]

    @pl.when(t == 0)
    def _():
        for k in range(2):
            hot[0, k] = one_hot(slot_own[k], rows)
            hot[1, k] = one_hot(slot_sib[k], rows)
            scale = row_probs(slot_own[k], prob[k], rows)
            scale_ref[rows * k : rows * (k + 1), :] = jnp.broadcast_to(scale, (rows, 128))
        gate[...] = jnp.zeros_like(gate)
        up[...] = jnp.zeros_like(up)

    def put(k, got):
        xs[rows * k : rows * (k + 1), :] = got.astype(BF16)

    pick_rows(t, half, hot, cat, own, sib, put)
    gate[...] += dot(xs[...], wg[...])
    up[...] += dot(xs[...], wu[...])
    keep_columns(t, place, half, xs, xi_ref)

    @pl.when(t == 2 * half - 1)
    def _():
        g, u = gate[...], up[...]
        s = jax.nn.sigmoid(g)
        sg = g * s
        hid_ref[...] = (sg * u).astype(BF16)
        sg_ref[...] = sg
        slope_ref[...] = u * s * (1.0 + g * (1.0 - s))


def cotangent_kernel(place, hot, scale, *refs, half):
    own, sib = refs[0:8], refs[8:16]
    wd, sg, slope, dd_ref, yi_ref, cat, ys, dh = refs[16:]
    t = pl.program_id(0)
    rows = hot.shape[2]

    @pl.when(t == 0)
    def _():
        dh[...] = jnp.zeros_like(dh)

    def put(k, got):
        at = slice(rows * k, rows * (k + 1))
        ys[at, :] = (got * scale[at, 0:1]).astype(BF16)

    pick_rows(t, half, hot, cat, own, sib, put)
    dh[...] += dot(ys[...], wd[...], NT)
    keep_columns(t, place, half, ys, yi_ref)

    @pl.when(t == 2 * half - 1)
    def _():
        dd_ref[0] = (dh[...] * slope[...]).astype(BF16)
        dd_ref[1] = (dh[...] * sg[...]).astype(BF16)


def whole(a):
    return pl.BlockSpec(a.shape, lambda *_: (0,) * a.ndim)


def ring_specs(own, tile, half):
    def spec(block, at):
        array, index = block
        return pl.BlockSpec((1, array.shape[1], tile), lambda t, s: (index, 0, at(t)))

    here = [spec(b, lambda t: jnp.minimum(t, half - 1)) for b in own]
    return here + [spec(b, lambda t: jnp.maximum(t - half, 0)) for b in own]


def hidden_rows(place, slot_own, slot_sib, prob, own, sib, wg, wu, rows, half=2):
    width, ff = wg.shape
    tile = width // (2 * half)
    toks = own[0][0].shape[1]
    total = 2 * rows
    w_in = pl.BlockSpec((tile, ff), lambda t, s: (tile_of(t, s[0], half), 0))
    const = lambda shape: pl.BlockSpec(shape, lambda t, s: (0,) * len(shape))
    outs = [((total, ff), BF16), ((total, ff), F32), ((total, ff), F32), ((total, width // 4), BF16)]
    outs += [((2, 2, rows, 4 * toks), BF16), ((total, 128), F32)]
    return pl.pallas_call(
        functools.partial(hidden_kernel, half=half),
        grid_spec=pltpu.PrefetchScalarGridSpec(
            num_scalar_prefetch=1,
            grid=(2 * half,),
            in_specs=[whole(slot_own), whole(slot_sib), whole(prob)] + ring_specs(own, tile, half) + [w_in, w_in],
            out_specs=[const(shape) for shape, _ in outs],
            scratch_shapes=[
                pltpu.VMEM((4 * toks, tile), BF16),
                pltpu.VMEM((total, tile), BF16),
                pltpu.VMEM((total, ff), F32),
                pltpu.VMEM((total, ff), F32),
            ],
        ),
        out_shape=[jax.ShapeDtypeStruct(shape, kind) for shape, kind in outs],
        compiler_params=pltpu.CompilerParams(vmem_limit_bytes=56 * 2**20),
        cost_estimate=pl.CostEstimate(
            flops=2 * total * width * ff * 2 + 2 * total * 4 * toks * width,
            bytes_accessed=2 * 2 * width * ff + 16 * toks * width,
            transcendentals=0,
        ),
        name="hidden_rows",
    )(place, slot_own, slot_sib, prob, *(b for b, _ in own + sib), wg, wu)


def cotangent_rows(place, hot, scale, own, sib, wd, sg, slope, rows, half=2):
    ff, width = wd.shape
    tile = width // (2 * half)
    toks = own[0][0].shape[1]
    total = 2 * rows
    w_out = pl.BlockSpec((ff, tile), lambda t, s: (0, tile_of(t, s[0], half)))
    const = lambda shape: pl.BlockSpec(shape, lambda t, s: (0,) * len(shape))
    outs = [((2, total, ff), BF16), ((total, width // 4), BF16)]
    return pl.pallas_call(
        functools.partial(cotangent_kernel, half=half),
        grid_spec=pltpu.PrefetchScalarGridSpec(
            num_scalar_prefetch=1,
            grid=(2 * half,),
            in_specs=[whole(hot), whole(scale)]
            + ring_specs(own, tile, half) + [w_out, whole(sg), whole(slope)],
            out_specs=[const(shape) for shape, _ in outs],
            scratch_shapes=[
                pltpu.VMEM((4 * toks, tile), BF16),
                pltpu.VMEM((total, tile), BF16),
                pltpu.VMEM((total, ff), F32),
            ],
        ),
        out_shape=[jax.ShapeDtypeStruct(shape, kind) for shape, kind in outs],
        compiler_params=pltpu.CompilerParams(vmem_limit_bytes=56 * 2**20),
        cost_estimate=pl.CostEstimate(
            flops=2 * total * width * ff + 2 * total * 4 * toks * width,
            bytes_accessed=2 * width * ff + 16 * toks * width,
            transcendentals=0,
        ),
        name="cotangent_rows",
    )(place, hot, scale, *(b for b, _ in own + sib), wd, sg, slope)


def rowgrad_kernel(h, wg, wu, out_ref, grad, pieces, *, cap):
    t = pl.program_id(0)
    devices = out_ref.shape[0]
    grad[...] = dot(h[0], wg[...], NT) + dot(h[1], wu[...], NT)
    for q in range(4):

        @pl.when(t == q)
        def _():
            for n in range(devices):
                at = cap * (n // 2 + devices // 2 * (n % 2))
                pieces[n, cap * q : cap * (q + 1), :] = grad[at : at + cap, :]

    @pl.when(t == 3)
    def _():
        out_ref[...] = pieces[...].astype(BF16)


def rowgrad(h, wg, wu, cap):
    width, ff = wg.shape
    rows = h.shape[1]
    devices, tile = rows // cap, width // 4
    w_in = pl.BlockSpec((tile, ff), lambda t: (t, 0))
    shape = (devices, 4 * cap, tile)
    return pl.pallas_call(
        functools.partial(rowgrad_kernel, cap=cap),
        grid=(4,),
        in_specs=[whole(h), w_in, w_in],
        out_specs=pl.BlockSpec(shape, lambda t: (0, 0, 0)),
        scratch_shapes=[pltpu.VMEM((rows, tile), F32), pltpu.VMEM(shape, F32)],
        out_shape=jax.ShapeDtypeStruct(shape, BF16),
        compiler_params=pltpu.CompilerParams(vmem_limit_bytes=56 * 2**20),
        cost_estimate=pl.CostEstimate(
            flops=2 * rows * width * ff * 2,
            bytes_accessed=2 * 2 * width * ff + 2 * rows * width,
            transcendentals=0,
        ),
        name="rowgrad",
    )(h, wg, wu)


def gather_kernel(slot, prob, xi, yi, blocks, out_ref, cat, xs, ys):
    i, j = pl.program_id(0), pl.program_id(1)
    total, wide = xi.shape
    chips, chunks, toks = blocks.shape[0], blocks.shape[1], blocks.shape[4]
    rows = total // chunks

    @pl.when((i == 0) & (j == 0))
    def _():
        xs[0:total] = xi[...]
        ys[0:total] = yi[...]

    @pl.when((i > 0) | (j > 0))
    def _():
        for k in range(chunks):
            slots = slot[0, k]
            hot = one_hot(slots, rows)
            scale = row_probs(slots, prob[0, k], rows)
            at = pl.ds(pl.multiple_of(j * total + k * rows, rows), rows)
            for n in range(chips):
                cat[toks * n : toks * (n + 1), :] = blocks[n, k, 0, 0]
            xs[at, :] = dot(hot, cat[...]).astype(BF16)
            for n in range(chips):
                cat[toks * n : toks * (n + 1), :] = blocks[n, k, 0, 1]
            ys[at, :] = (dot(hot, cat[...]) * scale).astype(BF16)

    @pl.when(j == 1)
    def _():
        out_ref[0:wide] = xs[...].T
        out_ref[wide:] = ys[...].T


def gather_columns(slot, prob, xi, yi, blocks):
    total, wide = xi.shape
    chips, chunks, _, _, toks, _ = blocks.shape
    meta = pl.BlockSpec((1, chunks, 1, chips * toks), lambda i, j: (2 * i + j, 0, 0, 0))
    return pl.pallas_call(
        gather_kernel,
        grid=(2, 2),
        in_specs=[
            meta, meta, whole(xi), whole(yi),
            pl.BlockSpec(
                (chips, chunks, 1, 2, toks, wide),
                lambda i, j: (0, 0, jnp.maximum(2 * i + j - 1, 0), 0, 0, 0),
            ),
        ],
        out_specs=pl.BlockSpec((2 * wide, 2 * total), lambda i, j: (0, i)),
        scratch_shapes=[
            pltpu.VMEM((chips * toks, wide), BF16),
            pltpu.VMEM((2 * total, wide), BF16),
            pltpu.VMEM((2 * total, wide), BF16),
        ],
        out_shape=jax.ShapeDtypeStruct((2 * wide, 4 * total), BF16),
        compiler_params=pltpu.CompilerParams(vmem_limit_bytes=56 * 2**20),
        cost_estimate=LIGHT,
        name="gather_columns",
    )(slot, prob, xi, yi, blocks)


def weight_kernel(xy, *refs, count, only):
    outs, cat = refs[-1 - count : -1], refs[-1]
    m = pl.program_id(0)
    at = 0
    for h, step_of in zip(refs[: -1 - count], only):
        rows = h.shape[-2]
        if step_of is None:
            cat[at : at + rows, :] = h[0] if h.ndim == 3 else h[...]
            at += rows
            continue

        @pl.when(m == step_of)
        def _(h=h, to=slice(at, at + rows)):
            cat[to, :] = h[...]

        if step_of == count - 1:
            at += rows
    res = dot(xy[...], cat[...]).astype(BF16)
    for i, out in enumerate(outs):

        @pl.when(m == i)
        def _():
            out[...] = res if out.shape == res.shape else res.T


def weights(xy, side, hs, count, flip):
    wide, depth = xy.shape[0] // 2, xy.shape[1]
    ff = hs[0][0].shape[-1]
    shape = (ff, wide) if flip else (wide, ff)

    def spec(block):
        array, rows, index = block[:3]
        if array.ndim == 3:
            return pl.BlockSpec((1, rows, ff), lambda m: (index(m), 0, 0))
        return pl.BlockSpec((rows, ff), lambda m: (index(m), 0))

    return pl.pallas_call(
        functools.partial(
            weight_kernel, count=count, only=[h[3] if len(h) > 3 else None for h in hs]
        ),
        grid=(count,),
        in_specs=[pl.BlockSpec((wide, depth), lambda m: (side, 0))] + [spec(h) for h in hs],
        out_specs=[pl.BlockSpec(shape, lambda m: (0, 0))] * count,
        scratch_shapes=[pltpu.VMEM((depth, ff), BF16)],
        out_shape=[jax.ShapeDtypeStruct(shape, BF16)] * count,
        compiler_params=pltpu.CompilerParams(vmem_limit_bytes=56 * 2**20),
        cost_estimate=pl.CostEstimate(
            flops=HEAVY * 2 * depth * wide * ff * count, bytes_accessed=depth * (2 * wide + 2 * ff * count), transcendentals=0
        ),
        name="weight_grads",
    )(xy, *(h[0] for h in hs))


def on_device(tokens, out_grad, expert_ids, route_probs, w_gate, w_up, w_down):
    toks, width = tokens.shape
    topk = expert_ids.shape[1]
    groups = lax.axis_size("expert")
    cap = 3 * toks * topk // (2 * groups)
    wg, wu, wd = w_gate[0], w_up[0], w_down[0]
    ff = wg.shape[1]
    rows = 16 * cap
    grp = lax.axis_index("dp")
    expert = lax.axis_index("expert")
    z, x, core = expert // 8, (expert // 2) % 4, expert % 2
    first = core == 0
    place = jnp.stack([core, grp]).astype(jnp.int32)
    both = jnp.stack([tokens, out_grad])

    def by_core(v):
        half = v.shape[-1] // 2
        mine = lax.dynamic_slice_in_dim(v, core * half, half, v.ndim - 1)
        other = lax.dynamic_slice_in_dim(v, (1 - core) * half, half, v.ndim - 1)
        got = swap_core(other)
        return jnp.where(first, mine, got), jnp.where(first, got, mine)

    named = expert_ids[:, :, None] == jnp.arange(groups, dtype=jnp.int32)
    chosen = jnp.any(named, axis=1)
    weight = jnp.sum(jnp.where(named, route_probs[:, :, None], 0.0), axis=1)
    lower = jnp.tril(jnp.ones((toks, toks), BF16), -1)
    rank = jnp.where(chosen, dot(lower, chosen.astype(BF16)), -1000.0)
    mine = jnp.stack(by_core(both), axis=1)
    blocks = (mine, *near(mine, 1), step(mine, 1, 2))
    col_x, col_y = (jnp.concatenate([b[v] for b in blocks], axis=-2) for v in (0, 1))

    meta = lax.all_to_all(jnp.stack([rank.T, weight.T], axis=1), "expert", 0, 0, tiled=True)
    col_x, col_y = after((col_x, col_y), meta)
    prev_x, succ_x = near(col_x, 2)

    quarter = width // 4
    part0 = lax.reduce_precision(meta[:, 1], 8, 7)
    part1 = lax.reduce_precision(meta[:, 1] - part0, 8, 7)
    part2 = meta[:, 1] - part0 - part1
    words = jnp.stack([meta[:, 0], part0, part1, part2]).astype(BF16)
    lines = words.size // quarter
    words = words.reshape(lines, quarter)
    cols, tables = [], [meta]
    for g in (1, 2, 3):
        r = 4 - g
        part = lax.dynamic_slice_in_dim(after(both, col_x), ((grp + r) % 4) * quarter, quarter, 2)
        part = jnp.concatenate([part.reshape(2 * toks, quarter), words])
        got = over_groups(part, r)
        cols.append(got[: 2 * toks])
        got = got[2 * toks :].reshape(4, groups, toks).astype(F32)
        tables.append(jnp.stack([got[0], got[1] + got[2] + got[3]], axis=1))
    cols = jnp.concatenate(cols)
    tables = jnp.stack(tables).reshape(4, 16, 2, 2, toks)
    base = cap * jnp.arange(16, dtype=jnp.int32)[:, None]
    slots = (tables[:, :, :, 0].astype(jnp.int32) + base[None, :, None]).swapaxes(1, 2)
    slots = slots.reshape(4, 2, 1, 16 * toks)
    probs = tables[:, :, :, 1].swapaxes(1, 2).reshape(4, 2, 1, 16 * toks)

    sib_near = (swap_core(col_x), swap_core(after(prev_x, cols)), swap_core(after(succ_x, cols)))
    ready = lambda v: after(v, sib_near)
    up = step(ready(jnp.concatenate([prev_x[:1], col_y])), 2, 1)
    down = step(ready(jnp.concatenate([succ_x[1:], col_y])), 2, -1)
    far_y = step(up[1:2], 2, 1), step(down[2:], 2, -1)

    def blocks_x(col, prev, succ, up, down):
        return [(col, 0), (prev, 0), (succ, 0), (up, 0), (col, 1), (prev, 1), (succ, 1), (down, 0)]

    def blocks_y(col, up, down, far0, far1):
        return [(col, 0), (up, 1), (down, 1), (far0, 0), (col, 1), (up, 2), (down, 2), (far1, 0)]

    sib_up, sib_down = swap_core(up), swap_core(down)
    own_x = blocks_x(col_x, prev_x, succ_x, up, down)
    sib_x = blocks_x(*sib_near, sib_up, sib_down)
    own_y = blocks_y(col_y, up, down, *far_y)

    table = meta.reshape(16, 2, 2, toks)
    offs = jnp.array(OFFSETS, jnp.int32)
    r2, r1 = offs[:, None], offs[None, :]
    bz = jnp.where(first, z + r1, z + r2) % 4
    bx = jnp.where(first, x + r2, x + r1) % 4
    chip = bz * 4 + bx
    order = jnp.concatenate([chip.reshape(16), chip.T.reshape(16)])
    local = table[order].reshape(2, 16, 2, 2, toks)
    local_slots = local[:, :, :, 0].astype(jnp.int32) + (cap * order).reshape(2, 16, 1, 1)
    local_slots = local_slots.swapaxes(1, 2).reshape(2, 2, 1, 16 * toks)
    local_probs = local[0, :, :, 1].swapaxes(0, 1).reshape(2, 1, 16 * toks)

    cols = lax.all_gather(after(cols, up, down), "expert", tiled=True)
    cols = cols.reshape(16, 2, 3, 2, toks, quarter)

    hid, sg, slope, xi, hot, scale = hidden_rows(
        place, local_slots[0], local_slots[1], local_probs, own_x, sib_x, wg, wu, rows
    )
    hid_prev, hid_succ = over_groups(hid, 1), over_groups(hid, -1)
    sib_far = [swap_core(after(b, hid)) for b in far_y]
    sib_y = blocks_y(swap_core(col_y), sib_up, sib_down, *sib_far)
    dd, yi = cotangent_rows(
        place, hot, scale, own_y, sib_y, wd, sg, slope, rows
    )

    half = hid.shape[0] // 2
    flat = dd.reshape(-1, ff)
    from_prev = over_groups(jnp.concatenate([hid_prev[:half], flat]), 1)
    from_succ = over_groups(jnp.concatenate([hid_succ[half:], flat]), -1)
    grad = rowgrad(dd, wg, wu, cap)
    xy = gather_columns(after(slots, grad), probs, xi, yi, cols)
    far_gate = over_groups(after(from_prev, xy)[half : 3 * half], 1)
    far_up = over_groups(after(from_succ, xy)[3 * half :], -1)

    back = lax.all_to_all(grad, "expert", 0, 0, tiled=True)
    at = lambda i: lambda m: i
    hids = [(hid, 2 * half, at(0)), (hid_succ, 2 * half, at(0)), (from_prev, half, at(0)),
            (from_succ, half, at(0)), (hid_prev, 2 * half, at(0))]
    (down_grad,) = weights(xy, 1, hids, 1, True)
    far_gate, far_up = after((far_gate, far_up), down_grad)
    first_half, second_half = (lambda m: 1 + 2 * m), (lambda m: 2 + 2 * m)
    dds = [(dd, 2 * half, lambda m: m), (from_succ, half, first_half), (from_succ, half, second_half),
           (far_gate, 2 * half, at(0), 0), (far_up, 2 * half, at(0), 1), (from_prev, half, first_half), (from_prev, half, second_half)]
    gate_grad, up_grad = weights(xy, 0, dds, 2, False)
    back = after(back, gate_grad)
    piece = cap * jnp.arange(4, dtype=F32)
    pick = after(rank, xy) + piece[:, None, None]
    pick = pick[..., None] == jnp.arange(4 * cap, dtype=F32)
    pick = pick.astype(BF16).reshape(4 * toks, groups * 4 * cap)
    token_grad = dot(pick, back.reshape(groups * 4 * cap, quarter)).astype(BF16)
    token_grad = token_grad.reshape(4, toks, quarter).swapaxes(0, 1).reshape(toks, width)

    return token_grad, gate_grad[None], up_grad[None], down_grad[None]


def solution(mesh):
    in_specs = (
        P(("dp", "expert"), None),
        P(("dp", "expert"), None),
        P(("dp", "expert"), None),
        P(("dp", "expert"), None),
        P("expert", None, None),
        P("expert", None, None),
        P("expert", None, None),
    )
    out_specs = (
        P(("dp", "expert"), None),
        P("expert", "dp", None),
        P("expert", "dp", None),
        P("expert", None, "dp"),
    )
    return jax.shard_map(
        on_device, mesh=mesh, in_specs=in_specs, out_specs=out_specs, check_vma=False
    )
```
